32 devices in a mesh: dp: 8 (over y, x, core), ctx: 4 (over z).
Axes of the slice: x: 2, y: 2, z: 4, core: 2. Of those that a mesh axis runs over, the one named last changes fastest.
Arguments:
- tokens: bfloat16 [16, 1024, 1024], P('dp', 'ctx'), may hold values from -6 to 6
- segments: int32 [16, 1024], P('dp'), may hold values from 0 to 6, as said below
- positions: int32 [16, 1024], P('dp', 'ctx'), may hold values from 0 to 1226, as said below
- attn_gain: bfloat16 [1024], P(('dp', 'ctx')), may hold values from 0.5 to 1.5
- w_query: bfloat16 [1024, 2048], P(('dp', 'ctx')), may hold values from -0.1875 to 0.1875
- w_key: bfloat16 [1024, 1024], P(('dp', 'ctx')), may hold values from -0.1875 to 0.1875
- w_value: bfloat16 [1024, 1024], P(('dp', 'ctx')), may hold values from -0.1875 to 0.1875
- w_out: bfloat16 [1024, 2048], P(('dp', 'ctx')), may hold values from -0.5 to 0.5
- qk_gain: bfloat16 [2, 128], replicated, may hold values from 0.25 to 1.75
- mlp_gain: bfloat16 [1024], P(('dp', 'ctx')), may hold values from 0.5 to 1.5
- w_gate: bfloat16 [1024, 3072], P(('dp', 'ctx')), may hold values from -0.1875 to 0.1875
- w_up: bfloat16 [1024, 3072], P(('dp', 'ctx')), may hold values from -0.1875 to 0.1875
- w_down: bfloat16 [1024, 3072], P(('dp', 'ctx')), may hold values from -0.21875 to 0.21875
- cotangent: bfloat16 [16, 1024, 1024], P('dp', 'ctx'), may hold values from -6 to 6
Outputs:
- layer_out: bfloat16 [16, 1024, 1024], P('dp', 'ctx')
- d_tokens: float32 [16, 1024, 1024], P('dp', 'ctx')
- d_attn_gain: float32 [1024], P(('dp', 'ctx'))
- d_w_query: float32 [1024, 2048], P(('dp', 'ctx'))
- d_w_key: float32 [1024, 1024], P(('dp', 'ctx'))
- d_w_value: float32 [1024, 1024], P(('dp', 'ctx'))
- d_w_out: float32 [1024, 2048], P(('dp', 'ctx'))
- d_qk_gain: float32 [2, 128], replicated
- d_mlp_gain: float32 [1024], P(('dp', 'ctx'))
- d_w_gate: float32 [1024, 3072], P(('dp', 'ctx'))
- d_w_up: float32 [1024, 3072], P(('dp', 'ctx'))
- d_w_down: float32 [1024, 3072], P(('dp', 'ctx'))
The draws below stay inside these ranges and needn't reach their ends.
Inputs may be any that keep to these rules, and one draw needn't show every extreme that they name: `segments`: numbers start at 0 in every sequence and rise by one at the first token of each further document; every document holds 204 tokens or more, counting those before the sequence, except the last document of a sequence, which may be cut off by its end. `positions`: A token's position counts from its document's first token; a sequence's first document may have begun up to 203 tokens before the sequence.
All inputs are finite; a program needn't handle non-finite values.
Results may differ from the reference program's by a relative error of at most 0.017.
Values may be sent and summed in bfloat16 or wider, within the bound.
No kernel may reach another device: no remote copies, remote signals or barrier semaphores. Data moves between devices by JAX's collectives and lax.ppermute only.
A program may use at most 256 MiB of HBM per device.

```python
import jax
import jax.numpy as jnp
from jax import lax

D = 1024
HQ = 16
HK = 8
DH = 128
FF = 3072
SEQ_LEN = 1024
SEQS_DEV = 2
SEQS = 16
STRETCH = 256


def layout(key):
    shortest = SEQ_LEN // 5
    slots_max = SEQ_LEN // shortest + 2
    key_len, key_off, key_pick, key_cut = jax.random.split(key, 4)
    groups = SEQS // SEQS_DEV
    chosen = jax.random.randint(key_pick, (groups, 1), 0, SEQS_DEV)
    member = jnp.arange(SEQS_DEV, dtype=jnp.int32)[None, :]
    single = (member == chosen).reshape(SEQS, 1)
    first_group = (jnp.arange(groups, dtype=jnp.int32) == 0)[:, None]
    packed_row = (first_group & (member == (chosen + 1) % SEQS_DEV) & (member != chosen)).reshape(SEQS, 1)
    pinned = (first_group & (member == chosen)).reshape(SEQS, 1)
    lengths = jax.random.randint(key_len, (SEQS, slots_max), shortest, SEQ_LEN + 1)
    lengths = jnp.where(packed_row, shortest, lengths)
    offset = jax.random.randint(key_off, (SEQS, 1), 0, shortest)
    offset = jnp.where(packed_row | pinned, shortest - 1, offset)
    doc_end = jnp.cumsum(lengths, axis=1) - offset
    doc_start = doc_end - lengths
    places = jnp.arange(SEQ_LEN, dtype=jnp.int32)
    numbers = jnp.sum((doc_end[:, None, :] <= places[None, :, None]).astype(jnp.int32), axis=2)
    begun = jnp.take_along_axis(doc_start, numbers, axis=1)
    tail = jax.random.randint(key_cut, (SEQS, 1), 1, STRETCH)
    tail = jnp.where(pinned, 0, tail)
    cut_at = SEQ_LEN - tail
    after_cut = places[None, :] >= cut_at
    single_numbers = after_cut.astype(jnp.int32)
    single_begun = jnp.where(after_cut, cut_at, -offset)
    numbers = jnp.where(single, single_numbers, numbers)
    begun = jnp.where(single, single_begun, begun)
    return (numbers.astype(jnp.int32), (places[None, :] - begun).astype(jnp.int32))


def draw_segments(key, part):
    numbers, placed = layout(key)
    return numbers


def draw_positions(key, part):
    numbers, placed = layout(key)
    return placed


def levels(rng, extent, shards, smallest, high):
    level, own = 1.0, jax.random.fold_in(rng, 6)
    for dim, parts in shards:
        heights = jnp.exp(jax.random.uniform(jax.random.fold_in(own, dim), (parts,), jnp.float32, smallest / len(shards), high / len(shards)))
        level = level * jnp.repeat(heights, extent[dim] // parts).reshape([-1 if axis == dim else 1 for axis in range(len(extent))])
    return level


def gaussian(key, dims, spread, bound, cuts=(), held_as=jnp.bfloat16):
    loudness = levels(key, dims, cuts, -0.22, 0.18) if cuts else 1.0
    values = jax.random.normal(key, dims, jnp.float32) * spread * loudness
    return jnp.minimum(jnp.maximum(values, -bound), bound).astype(held_as)


def setup_inputs(seed: int = 0) -> dict:
    key_list = jax.random.split(jax.random.key(seed), 15)
    tokens = gaussian(key_list[0], (SEQS, SEQ_LEN, D), 1.0, 6.0, ((0, 8), (1, 4)))
    segments = draw_segments(jax.random.fold_in(key_list[14], 71), 0)
    positions = draw_positions(jax.random.fold_in(key_list[14], 71), 0)
    attn_gain = jnp.clip(1.0 + 0.1 * jax.random.normal(key_list[3], (D,), jnp.float32), 0.5, 1.5).astype(jnp.bfloat16)
    w_query = gaussian(key_list[4], (D, HQ * DH), D ** -0.5, 0.1875, ((0, 32),))
    w_key = gaussian(key_list[5], (D, HK * DH), D ** -0.5, 0.1875, ((0, 32),))
    w_value = gaussian(key_list[6], (D, HK * DH), D ** -0.5, 0.1875, ((0, 32),))
    w_out = gaussian(key_list[7], (D, HQ * DH), (HQ * DH // 16) ** -0.5, 0.5, ((0, 32),))
    qk_gain = jnp.clip(1.0 + 0.15 * jax.random.normal(key_list[8], (2, DH), jnp.float32), 0.25, 1.75).astype(jnp.bfloat16)
    mlp_gain = jnp.clip(1.0 + 0.1 * jax.random.normal(key_list[9], (D,), jnp.float32), 0.5, 1.5).astype(jnp.bfloat16)
    w_gate = gaussian(key_list[10], (D, FF), D ** -0.5, 0.1875, ((0, 32),))
    w_up = gaussian(key_list[11], (D, FF), D ** -0.5, 0.1875, ((0, 32),))
    w_down = gaussian(key_list[12], (D, FF), (FF // 4) ** -0.5, 0.21875, ((0, 32),))
    cotangent = gaussian(key_list[13], (SEQS, SEQ_LEN, D), 1.0, 6.0, ((0, 8), (1, 4)))
    return dict(tokens=tokens, segments=segments, positions=positions, attn_gain=attn_gain, w_query=w_query, w_key=w_key, w_value=w_value, w_out=w_out, qk_gain=qk_gain, mlp_gain=mlp_gain, w_gate=w_gate, w_up=w_up, w_down=w_down, cotangent=cotangent)


norm_eps = 1e-06
rope_base = 1000000.0

@jax.custom_vjp
def low(v):
    return lax.optimization_barrier(v.astype(jnp.bfloat16)).astype(jnp.float32)

@jax.custom_vjp
def low_back(v):
    return v

def low_keep(v):
    return (low(v), None)

def low_pass(kept, grad):
    return (grad,)

def back_keep(v):
    return (v, None)

def back_low(kept, grad):
    return (low(grad),)
low.defvjp(low_keep, low_pass)
low_back.defvjp(back_keep, back_low)

def hi_dot(left, right):
    return jnp.dot(left, right, precision=lax.Precision.HIGHEST)

def norm_scale(values, gain):
    return values * lax.rsqrt(lax.optimization_barrier(jnp.mean(values * values, axis=-1, keepdims=True)) + norm_eps) * gain

def rotate(values, positions):
    half_dim = values.shape[-1] // 2
    inv_freq = rope_base ** (-2.0 * jnp.arange(half_dim, dtype=jnp.float32) / values.shape[-1])
    angles = positions.astype(jnp.float32)[..., None, None] * inv_freq
    cosine = jnp.cos(angles)
    sine = jnp.sin(angles)
    first_half = values[..., :half_dim]
    second_half = values[..., half_dim:]
    return jnp.concatenate([first_half * cosine - second_half * sine, second_half * cosine + first_half * sine], axis=-1)

def attend(queries, keys, values, segment_row):
    length = queries.shape[0]
    heads_per = HQ // HK
    grouped = queries.reshape(length, HK, heads_per, DH)
    scores = jnp.einsum('qhgd,khd->hgqk', grouped, keys, precision=lax.Precision.HIGHEST) * DH ** (-0.5)
    scores = low_back(scores)
    places = jnp.arange(length, dtype=jnp.int32)
    visible = (segment_row[:, None] == segment_row[None, :]) & (places[None, :] <= places[:, None])
    scores = jnp.where(visible, scores, -1e+30)
    row_max = lax.optimization_barrier(jnp.max(scores, axis=-1, keepdims=True))
    weights = jnp.exp(scores - row_max)
    prob_low = low(weights / lax.optimization_barrier(jnp.sum(weights, axis=-1, keepdims=True)))
    attn_mix = jnp.einsum('hgqk,khd->qhgd', prob_low, values, precision=lax.Precision.HIGHEST)
    return attn_mix.reshape(length, HQ * DH)

def attend_item(group_item):
    return attend(group_item[0], group_item[1], group_item[2], group_item[3])

def block_forward(weights, inputs, seg_rows, pos_rows):
    attn_gain, w_query, w_key, w_value, w_out, qk_gain, mlp_gain, w_gate, w_up, w_down = weights
    seq_count = inputs.shape[0]
    token_count = seq_count * SEQ_LEN
    resid_in = inputs.reshape(token_count, D)
    normed = low(norm_scale(resid_in, attn_gain))
    q_proj = low_back(hi_dot(normed, w_query)).reshape(seq_count, SEQ_LEN, HQ, DH)
    k_proj = low_back(hi_dot(normed, w_key)).reshape(seq_count, SEQ_LEN, HK, DH)
    v_low = low(low_back(hi_dot(normed, w_value))).reshape(seq_count, SEQ_LEN, HK, DH)
    q_low = low(rotate(norm_scale(q_proj, qk_gain[0]), pos_rows))
    k_low = low(rotate(norm_scale(k_proj, qk_gain[1]), pos_rows))
    attn_mix = lax.map(jax.checkpoint(attend_item), (q_low, k_low, v_low, seg_rows))
    attn_mix = low(low_back(attn_mix.reshape(token_count, HQ * DH)))
    hidden_in = resid_in + low_back(hi_dot(attn_mix, w_out.T))
    normed_mlp = low(norm_scale(hidden_in, mlp_gain))
    gated = low_back(hi_dot(normed_mlp, w_gate))
    upward = low_back(hi_dot(normed_mlp, w_up))
    inner = low(jax.nn.silu(gated) * upward)
    result = hidden_in + low_back(hi_dot(inner, w_down.T))
    return result.reshape(seq_count, SEQ_LEN, D)

def reference(tokens, segments, positions, attn_gain, w_query, w_key, w_value, w_out, qk_gain, mlp_gain, w_gate, w_up, w_down, cotangent):
    weights = tuple((source.astype(jnp.float32) for source in (attn_gain, w_query, w_key, w_value, w_out, qk_gain, mlp_gain, w_gate, w_up, w_down)))
    group_count = SEQS // SEQS_DEV
    inputs = tokens.astype(jnp.float32).reshape(group_count, SEQS_DEV, SEQ_LEN, D)
    seg_groups = segments.reshape(group_count, SEQS_DEV, SEQ_LEN)
    pos_groups = positions.reshape(group_count, SEQS_DEV, SEQ_LEN)

    def forward(weights, inputs):

        def scan_step(carry, group_item):
            return (carry, jax.checkpoint(block_forward)(weights, group_item[0], group_item[1], group_item[2]))
        carry, results = lax.scan(scan_step, None, (inputs, seg_groups, pos_groups))
        return results
    results, pullback = jax.vjp(forward, weights, inputs)
    weight_grads, input_grads = pullback(cotangent.astype(jnp.float32).reshape(inputs.shape))
    layer_out = results.reshape(SEQS, SEQ_LEN, D).astype(jnp.bfloat16)
    d_tokens = input_grads.reshape(SEQS, SEQ_LEN, D)
    return (layer_out, d_tokens, weight_grads[0], weight_grads[1], weight_grads[2], weight_grads[3], weight_grads[4], weight_grads[5], weight_grads[6], weight_grads[7], weight_grads[8], weight_grads[9])
```

```python
import functools
import math

import jax
import jax.numpy as jnp
from jax import lax
from jax.experimental import pallas as pl
from jax.experimental.pallas import tpu as pltpu
from jax.sharding import PartitionSpec as P

D = 1024
HQ = 16
HK = 8
DH = 128


norm_eps = 1e-06
rope_base = 1000000.0


def norm_rows(values, gain):
    factor = lax.rsqrt(jnp.mean(values * values, axis=-1, keepdims=True) + norm_eps)
    return (values * factor * gain, factor)


def norm_back(values, factor, gain, upstream):
    weighted = upstream * gain
    lead_axes = tuple(range(values.ndim - 1))
    gain_grad = jnp.sum(upstream * values * factor, axis=lead_axes)
    inner_mean = jnp.mean(weighted * values, axis=-1, keepdims=True)
    return (gain_grad, factor * weighted - values * factor * factor * factor * inner_mean)


def rotate(values, positions, sign):
    half_dim = values.shape[-1] // 2
    inv_freq = rope_base ** (-2.0 * jnp.arange(half_dim, dtype=jnp.float32) / values.shape[-1])
    angles = positions.astype(jnp.float32)[:, None, None] * inv_freq
    cosine = jnp.cos(angles)
    sine = sign * jnp.sin(angles)
    first_half = values[..., :half_dim]
    second_half = values[..., half_dim:]
    return jnp.concatenate(
        [first_half * cosine - second_half * sine, second_half * cosine + first_half * sine],
        axis=-1,
    )


def visibility(segment_row, q_first, span_len):
    key_places = jnp.arange(segment_row.shape[0], dtype=jnp.int32)
    query_places = q_first + jnp.arange(span_len, dtype=jnp.int32)
    query_segs = lax.dynamic_slice_in_dim(segment_row, q_first, span_len)
    return (query_segs[:, None] == segment_row[None, :]) & (
        key_places[None, :] <= query_places[:, None]
    )


def masked_scores(grouped, keys, visible):
    scores = jnp.einsum(
        "qhgd,khd->hgqk", grouped, keys, preferred_element_type=jnp.float32
    ) * DH ** (-0.5)
    return jnp.where(visible, scores, -1e30)


def local(
    tokens,
    segments,
    positions,
    attn_gain,
    w_query,
    w_key,
    w_value,
    w_out,
    qk_gain,
    mlp_gain,
    w_gate,
    w_up,
    w_down,
    cotangent,
):
    seq_count, span_len, _ = tokens.shape
    row_count = seq_count * span_len
    heads_per = HQ // HK
    q_first = lax.axis_index("ctx") * span_len
    pos_flat = positions.reshape(row_count)
    g_attn, wq_full, wk_full, wv_full, wo_full = (
        lax.all_gather(attn_gain, ("dp", "ctx"), axis=0, tiled=True),
        lax.all_gather(w_query, ("dp", "ctx"), axis=0, tiled=True),
        lax.all_gather(w_key, ("dp", "ctx"), axis=0, tiled=True),
        lax.all_gather(w_value, ("dp", "ctx"), axis=0, tiled=True),
        lax.all_gather(w_out, ("dp", "ctx"), axis=0, tiled=True),
    )
    resid_in = tokens.reshape(row_count, D).astype(jnp.float32)
    normed_f, factor_in = norm_rows(resid_in, g_attn.astype(jnp.float32))
    normed = normed_f.astype(jnp.bfloat16)
    q_proj = jnp.dot(normed, wq_full, preferred_element_type=jnp.float32).reshape(row_count, HQ, DH)
    k_proj = jnp.dot(normed, wk_full, preferred_element_type=jnp.float32).reshape(row_count, HK, DH)
    v_low = (
        jnp.dot(normed, wv_full, preferred_element_type=jnp.float32)
        .astype(jnp.bfloat16)
        .reshape(seq_count, span_len, HK, DH)
    )
    gains_qk = qk_gain.astype(jnp.float32)
    q_norm, factor_q = norm_rows(q_proj, gains_qk[0])
    k_norm, factor_k = norm_rows(k_proj, gains_qk[1])
    q_low = rotate(q_norm, pos_flat, 1.0).astype(jnp.bfloat16).reshape(seq_count, span_len, HQ, DH)
    k_low = rotate(k_norm, pos_flat, 1.0).astype(jnp.bfloat16).reshape(seq_count, span_len, HK, DH)
    keys_all, values_all = (
        lax.all_gather(k_low, "ctx", axis=1, tiled=True),
        lax.all_gather(v_low, "ctx", axis=1, tiled=True),
    )

    def attend_forward(group_item):
        queries, keys, values, segment_row = group_item
        visible = visibility(segment_row, q_first, span_len)
        grouped = queries.reshape(span_len, HK, heads_per, DH)
        scores = masked_scores(grouped, keys, visible)
        row_max = jnp.max(scores, axis=-1, keepdims=True)
        weights = jnp.exp(scores - row_max)
        row_total = jnp.sum(weights, axis=-1, keepdims=True)
        prob_low = (weights / row_total).astype(jnp.bfloat16)
        attn_mix = jnp.einsum(
            "hgqk,khd->qhgd", prob_low, values, preferred_element_type=jnp.float32
        )
        return (
            attn_mix.reshape(span_len, HQ * DH).astype(jnp.bfloat16),
            row_max + jnp.log(row_total),
        )

    attn_mix, log_total = lax.map(attend_forward, (q_low, keys_all, values_all, segments))
    attn_mix = attn_mix.reshape(row_count, HQ * DH)
    hidden_in = resid_in + jnp.einsum(
        "th,dh->td", attn_mix, wo_full, preferred_element_type=jnp.float32
    )
    g_mlp, wg_full, wu_full, wd_full = (
        lax.all_gather(mlp_gain, ("dp", "ctx"), axis=0, tiled=True),
        lax.all_gather(w_gate, ("dp", "ctx"), axis=0, tiled=True),
        lax.all_gather(w_up, ("dp", "ctx"), axis=0, tiled=True),
        lax.all_gather(w_down, ("dp", "ctx"), axis=0, tiled=True),
    )
    normed_mlp_f, factor_mlp = norm_rows(hidden_in, g_mlp.astype(jnp.float32))
    normed_mlp = normed_mlp_f.astype(jnp.bfloat16)
    gated = jnp.dot(normed_mlp, wg_full, preferred_element_type=jnp.float32)
    upward = jnp.dot(normed_mlp, wu_full, preferred_element_type=jnp.float32)
    sigmoid_gate = jax.nn.sigmoid(gated)
    silu_gate = gated * sigmoid_gate
    inner = (silu_gate * upward).astype(jnp.bfloat16)
    result = hidden_in + jnp.einsum("tf,df->td", inner, wd_full, preferred_element_type=jnp.float32)
    layer_out = result.astype(jnp.bfloat16).reshape(seq_count, span_len, D)
    g_mlp, wg_full, wu_full, wd_full = (
        lax.all_gather(mlp_gain, ("dp", "ctx"), axis=0, tiled=True),
        lax.all_gather(w_gate, ("dp", "ctx"), axis=0, tiled=True),
        lax.all_gather(w_up, ("dp", "ctx"), axis=0, tiled=True),
        lax.all_gather(w_down, ("dp", "ctx"), axis=0, tiled=True),
    )
    grad_out = cotangent.reshape(row_count, D)
    grad_inner = jnp.dot(grad_out, wd_full, preferred_element_type=jnp.float32)
    grad_gate = (grad_inner * upward * sigmoid_gate * (1.0 + gated * (1.0 - sigmoid_gate))).astype(
        jnp.bfloat16
    )
    grad_up = (grad_inner * silu_gate).astype(jnp.bfloat16)
    grad_normed_mlp = jnp.einsum(
        "tf,df->td", grad_gate, wg_full, preferred_element_type=jnp.float32
    )
    grad_normed_mlp = grad_normed_mlp + jnp.einsum(
        "tf,df->td", grad_up, wu_full, preferred_element_type=jnp.float32
    )
    mlp_gain_part, grad_resid_mlp = norm_back(
        hidden_in, factor_mlp, g_mlp.astype(jnp.float32), grad_normed_mlp
    )
    d_w_down = jnp.einsum("td,tf->df", grad_out, inner, preferred_element_type=jnp.float32)
    d_w_gate = jnp.einsum("td,tf->df", normed_mlp, grad_gate, preferred_element_type=jnp.float32)
    d_w_up = jnp.einsum("td,tf->df", normed_mlp, grad_up, preferred_element_type=jnp.float32)
    d_mlp_gain, d_w_gate, d_w_up, d_w_down = (
        lax.psum_scatter(mlp_gain_part, ("dp", "ctx"), scatter_dimension=0, tiled=True),
        lax.psum_scatter(d_w_gate, ("dp", "ctx"), scatter_dimension=0, tiled=True),
        lax.psum_scatter(d_w_up, ("dp", "ctx"), scatter_dimension=0, tiled=True),
        lax.psum_scatter(d_w_down, ("dp", "ctx"), scatter_dimension=0, tiled=True),
    )
    grad_hidden = grad_out.astype(jnp.float32) + grad_resid_mlp
    g_attn, wq_full, wk_full, wv_full, wo_full = (
        lax.all_gather(attn_gain, ("dp", "ctx"), axis=0, tiled=True),
        lax.all_gather(w_query, ("dp", "ctx"), axis=0, tiled=True),
        lax.all_gather(w_key, ("dp", "ctx"), axis=0, tiled=True),
        lax.all_gather(w_value, ("dp", "ctx"), axis=0, tiled=True),
        lax.all_gather(w_out, ("dp", "ctx"), axis=0, tiled=True),
    )
    grad_attn = grad_hidden.astype(jnp.bfloat16)
    grad_mix = jnp.einsum(
        "td,dh->th", grad_attn, wo_full, preferred_element_type=jnp.float32
    ).astype(jnp.bfloat16)
    grad_mix = grad_mix.reshape(seq_count, span_len, HQ, DH)

    def attend_backward(group_item):
        queries, keys, values, grad_rows, log_rows, segment_row = group_item
        visible = visibility(segment_row, q_first, span_len)
        grouped = queries.reshape(span_len, HK, heads_per, DH)
        scores = masked_scores(grouped, keys, visible)
        probs = jnp.exp(scores - log_rows)
        grad_group = grad_rows.reshape(span_len, HK, heads_per, DH)
        grad_probs = jnp.einsum(
            "qhgd,khd->hgqk", grad_group, values, preferred_element_type=jnp.float32
        )
        center = jnp.sum(probs * grad_probs, axis=-1, keepdims=True)
        grad_scores = (probs * (grad_probs - center)).astype(jnp.bfloat16)
        grad_q = jnp.einsum(
            "hgqk,khd->qhgd", grad_scores, keys, preferred_element_type=jnp.float32
        ) * DH ** (-0.5)
        grad_k = jnp.einsum(
            "hgqk,qhgd->khd", grad_scores, grouped, preferred_element_type=jnp.float32
        ) * DH ** (-0.5)
        grad_v = jnp.einsum(
            "hgqk,qhgd->khd",
            probs.astype(jnp.bfloat16),
            grad_group,
            preferred_element_type=jnp.float32,
        )
        return (grad_q.reshape(span_len, HQ, DH), grad_k, grad_v)

    grad_q, grad_k_all, grad_v_all = lax.map(
        attend_backward, (q_low, keys_all, values_all, grad_mix, log_total, segments)
    )
    grad_k, grad_v = (
        lax.psum_scatter(
            grad_k_all.astype(jnp.bfloat16), "ctx", scatter_dimension=1, tiled=True
        ).astype(jnp.float32),
        lax.psum_scatter(
            grad_v_all.astype(jnp.bfloat16), "ctx", scatter_dimension=1, tiled=True
        ).astype(jnp.float32),
    )
    grad_qn = rotate(grad_q.reshape(row_count, HQ, DH), pos_flat, -1.0)
    grad_kn = rotate(grad_k.reshape(row_count, HK, DH), pos_flat, -1.0)
    q_gain_part, grad_qp = norm_back(q_proj, factor_q, gains_qk[0], grad_qn)
    k_gain_part, grad_kp = norm_back(k_proj, factor_k, gains_qk[1], grad_kn)
    grad_q_low = grad_qp.reshape(row_count, HQ * DH).astype(jnp.bfloat16)
    grad_k_low = grad_kp.reshape(row_count, HK * DH).astype(jnp.bfloat16)
    grad_v_low = grad_v.reshape(row_count, HK * DH).astype(jnp.bfloat16)
    grad_normed = jnp.einsum("th,dh->td", grad_q_low, wq_full, preferred_element_type=jnp.float32)
    grad_normed = grad_normed + jnp.einsum(
        "th,dh->td", grad_k_low, wk_full, preferred_element_type=jnp.float32
    )
    grad_normed = grad_normed + jnp.einsum(
        "th,dh->td", grad_v_low, wv_full, preferred_element_type=jnp.float32
    )
    attn_gain_part, grad_resid_attn = norm_back(
        resid_in, factor_in, g_attn.astype(jnp.float32), grad_normed
    )
    d_qk_gain = lax.psum(jnp.stack([q_gain_part, k_gain_part]), ("dp", "ctx"))
    d_w_out = jnp.einsum("td,th->dh", grad_attn, attn_mix, preferred_element_type=jnp.float32)
    d_w_query = jnp.einsum("td,th->dh", normed, grad_q_low, preferred_element_type=jnp.float32)
    d_w_key = jnp.einsum("td,th->dh", normed, grad_k_low, preferred_element_type=jnp.float32)
    d_w_value = jnp.einsum("td,th->dh", normed, grad_v_low, preferred_element_type=jnp.float32)
    d_attn_gain, d_w_query, d_w_key, d_w_value, d_w_out = (
        lax.psum_scatter(attn_gain_part, ("dp", "ctx"), scatter_dimension=0, tiled=True),
        lax.psum_scatter(d_w_query, ("dp", "ctx"), scatter_dimension=0, tiled=True),
        lax.psum_scatter(d_w_key, ("dp", "ctx"), scatter_dimension=0, tiled=True),
        lax.psum_scatter(d_w_value, ("dp", "ctx"), scatter_dimension=0, tiled=True),
        lax.psum_scatter(d_w_out, ("dp", "ctx"), scatter_dimension=0, tiled=True),
    )
    d_tokens = (grad_hidden + grad_resid_attn).reshape(seq_count, span_len, D)
    return (
        layer_out,
        d_tokens,
        d_attn_gain,
        d_w_query,
        d_w_key,
        d_w_value,
        d_w_out,
        d_qk_gain,
        d_mlp_gain,
        d_w_gate,
        d_w_up,
        d_w_down,
    )


AXES = ("dp", "ctx")
SCALE = DH ** (-0.5)
LOG2E = math.log2(math.e)
NEG = -1e30
BF = jnp.bfloat16
F32 = jnp.float32


class Place:
    def __init__(self, dp_size, ctx_size):
        self.count = dp_size * ctx_size
        self.z_size = ctx_size
        dp = lax.axis_index("dp")
        self.z = lax.axis_index("ctx")
        self.c = dp % 2
        self.x = (dp // 2) % 2
        self.y = dp // 4

    def split(self, flat):
        z, dp = flat % self.z_size, flat // self.z_size
        return dp // 4, (dp // 2) % 2, dp % 2, z

    def join(self, y, x, c, z):
        return ((y * 2 + x) * 2 + c) * self.z_size + z

    def move(self, values, target):
        perm = []
        for flat in range(self.count):
            perm.append((flat, self.join(*target(*self.split(flat)))))
        return lax.ppermute(values, AXES, perm)

    def swap(self, values, axis):
        return self.move(
            values,
            lambda y, x, c, z: (
                1 - y if axis == "y" else y,
                1 - x if axis == "x" else x,
                1 - c if axis == "c" else c,
                z,
            ),
        )

    def shift(self, values, step):
        return self.move(values, lambda y, x, c, z: (y, x, c, (z + step) % self.z_size))


def after(values, *others):
    return lax.optimization_barrier((values,) + tuple(others))[0]


STRETCHES = ((0, 3), (1, 2))
CORE_OF = (0, 1, 1, 0)
RANK_OF = (0, 0, 1, 1)


def rank_here(place):
    return jnp.asarray(RANK_OF, jnp.int32)[place.z]


def to_sequences(place, values):
    parts = []
    rank = rank_here(place)
    for m in range(2):
        chosen = lax.dynamic_index_in_dim(values, (rank + m) % 2, 0, keepdims=False)
        parts.append(
            place.move(
                chosen, lambda y, x, c, z: (y, x, CORE_OF[z], 2 * c + (RANK_OF[z] + m) % 2)
            )
        )
    first, second = parts
    even = place.z % 2 == 0
    return jnp.concatenate(
        [jnp.where(even, first, second), jnp.where(even, second, first)], axis=0
    )


def from_sequences(place, values):
    parts = []
    for m in range(2):
        chosen = lax.dynamic_index_in_dim(values, (m + place.z) % 2, 0, keepdims=False)
        parts.append(
            place.move(
                chosen,
                lambda y, x, c, z: (y, x, z // 2, STRETCHES[c][(m + z) % 2]),
            )
        )
    first, second = parts
    even = rank_here(place) == 0
    return jnp.stack([jnp.where(even, first, second), jnp.where(even, second, first)])


def gather_z(place, shard):
    pieces = [shard] + [place.shift(shard, k) for k in range(1, place.z_size)]
    return jnp.stack(pieces)


def gather_rest(place, stacked, first_axis, second_axis):
    both = jnp.stack([stacked, place.swap(stacked, first_axis)])
    other = place.swap(both, second_axis)
    return both, other, place.swap(both, "c"), place.swap(other, "c")


def assemble(place, quarters, second_axis, widths):
    z_size, rows, total = place.z_size, quarters[0].shape[2], quarters[0].shape[3]
    first_is_x = second_axis == "y"
    here = jnp.stack(
        [place.x if first_is_x else place.y, place.y if first_is_x else place.x, place.c, place.z]
    ).astype(jnp.int32)

    def kernel(here_ref, near, far, near_core, far_core, *outs):
        second, core = here_ref[1], here_ref[2]
        for ref, from_second, from_core in (
            (near, 0, 0),
            (far, 1, 0),
            (near_core, 0, 1),
            (far_core, 1, 1),
        ):
            at_second = lax.rem(second + from_second, 2)
            at_core = lax.rem(core + from_core, 2)
            start = 0
            for out, width in zip(outs, widths):
                block = ref[0, 0, :, start : start + width]
                if first_is_x:
                    out[at_second, 0, at_core, 0] = block
                else:
                    out[0, at_second, at_core, 0] = block
                start += width

    def in_map(i, k, here_ref):
        return (i, k, 0, 0)

    def out_map(i, k, here_ref):
        first = lax.rem(here_ref[0] + i, 2)
        z = lax.rem(here_ref[3] + z_size - k, z_size)
        return (0, first, 0, z, 0, 0) if first_is_x else (first, 0, 0, z, 0, 0)

    def out_block(width):
        return (2, 1, 2, 1, rows, width) if first_is_x else (1, 2, 2, 1, rows, width)

    outs = pl.pallas_call(
        kernel,
        grid_spec=pltpu.PrefetchScalarGridSpec(
            num_scalar_prefetch=1,
            grid=(2, z_size),
            in_specs=[pl.BlockSpec((1, 1, rows, total), in_map)] * 4,
            out_specs=[pl.BlockSpec(out_block(width), out_map) for width in widths],
        ),
        out_shape=[
            jax.ShapeDtypeStruct((2, 2, 2, z_size, rows, width), BF) for width in widths
        ],
        compiler_params=pltpu.CompilerParams(vmem_limit_bytes=32 * 2**20),
        cost_estimate=pl.CostEstimate(
            flops=0, bytes_accessed=2 * 8 * z_size * rows * total * 2, transcendentals=0
        ),
        name="assemble",
    )(here, *quarters)
    return [out.reshape(8 * z_size * rows, out.shape[-1]) for out in outs]


def add_low(left, right):
    return (left.astype(F32) + right.astype(F32)).astype(BF)


def pick(values, index, axis):
    return lax.dynamic_index_in_dim(values, index, axis, keepdims=False)


def reduce_rows(place, grad, first_axis):
    rows, width = grad.shape[0] // place.count, grad.shape[1]
    parts = grad.reshape(2, 2, 2, place.z_size, rows, width)
    parts = add_low(pick(parts, place.c, 2), place.swap(pick(parts, 1 - place.c, 2), "c"))
    if first_axis == "y":
        steps = (("y", place.y, 0), ("x", place.x, 0))
    else:
        steps = (("x", place.x, 1), ("y", place.y, 0))
    for axis, index, dim in steps:
        received = place.swap(pick(parts, 1 - index, dim), axis)
        parts = add_low(pick(parts, index, dim), received)
    total = pick(parts, place.z, 0).astype(F32)
    for k in range(1, place.z_size):
        sent = pick(parts, (place.z + k) % place.z_size, 0)
        total = total + place.shift(sent, k).astype(F32)
    return total


def head_factor(values):
    return lax.rsqrt(jnp.mean(values * values, axis=-1, keepdims=True) + norm_eps)


def head_back(values, gain, upstream):
    factor = head_factor(values)
    weighted = upstream * gain
    gain_grad = jnp.sum(upstream * values * factor, axis=0, keepdims=True)
    inner_mean = jnp.mean(weighted * values, axis=-1, keepdims=True)
    return gain_grad, factor * weighted - values * factor * factor * factor * inner_mean


def turn(values, cosine, sine):
    return values * cosine + pltpu.roll(values, DH // 2, 1) * sine


def prepare_kv(kv_proj, gain, cosine, sine):
    rows = kv_proj.shape[0]

    def kernel(k_ref, v_ref, gain_ref, cos_ref, sin_ref, out_ref):
        values = k_ref[...]
        normed = values * head_factor(values) * gain_ref[...]
        out_ref[0] = turn(normed, cos_ref[...], sin_ref[...]).astype(BF)
        out_ref[1] = v_ref[...].astype(BF)

    whole = lambda shape: pl.BlockSpec(shape, lambda h: (0, 0))
    return pl.pallas_call(
        kernel,
        grid=(HK,),
        in_specs=[
            pl.BlockSpec((rows, DH), lambda h: (0, h)),
            pl.BlockSpec((rows, DH), lambda h: (0, HK + h)),
            whole((1, DH)),
            whole((rows, DH)),
            whole((rows, DH)),
        ],
        out_specs=pl.BlockSpec((2, rows, DH), lambda h: (0, 0, h)),
        out_shape=jax.ShapeDtypeStruct((2, rows, HK * DH), BF),
        cost_estimate=pl.CostEstimate(
            flops=10 * rows * HK * DH, bytes_accessed=12 * rows * HK * DH, transcendentals=0
        ),
        name="prepare_kv",
    )(kv_proj, kv_proj, gain, cosine, sine)


def finish_kv(kv_proj, own, received, gain, cosine, sine):
    rows = kv_proj.shape[0]

    def kernel(k_ref, own_ref, other_ref, gain_ref, cos_ref, sin_ref, out_ref, gain_out):
        @pl.when(pl.program_id(0) == 0)
        def _():
            gain_out[...] = jnp.zeros_like(gain_out)

        grad_k = own_ref[0] + other_ref[0].astype(F32)
        grad_kn = turn(grad_k, cos_ref[...], -sin_ref[...])
        gain_grad, grad_kp = head_back(k_ref[...], gain_ref[...], grad_kn)
        gain_out[...] += gain_grad
        out_ref[0] = grad_kp.astype(BF)
        out_ref[1] = (own_ref[1] + other_ref[1].astype(F32)).astype(BF)

    whole = lambda shape: pl.BlockSpec(shape, lambda h: (0, 0))
    pair = pl.BlockSpec((2, rows, DH), lambda h: (0, 0, h))
    return pl.pallas_call(
        kernel,
        grid=(HK,),
        in_specs=[
            pl.BlockSpec((rows, DH), lambda h: (0, h)),
            pair,
            pair,
            whole((1, DH)),
            whole((rows, DH)),
            whole((rows, DH)),
        ],
        out_specs=[pair, whole((1, DH))],
        out_shape=[
            jax.ShapeDtypeStruct((2, rows, HK * DH), BF),
            jax.ShapeDtypeStruct((1, DH), F32),
        ],
        cost_estimate=pl.CostEstimate(
            flops=30 * rows * HK * DH, bytes_accessed=20 * rows * HK * DH, transcendentals=0
        ),
        name="finish_kv",
    )(kv_proj, own, received, gain, cosine, sine)


def interleave(own, other):
    half = own.shape[0] // 2
    return jnp.concatenate([own[:half], other[:half], own[half:], other[half:]], axis=0)


def fill_bias(q_ref, k_ref, bias_ref):
    bias_ref[...] = jnp.where(
        (k_ref[:, 0:1] <= q_ref[0:1, :]) & (k_ref[:, 1:2] == q_ref[1:2, :]), 0.0, NEG
    ).astype(F32)


NT = (((1,), (1,)), ((), ()))
NN = (((1,), (0,)), ((), ()))


def dot32(left, right, dims):
    return lax.dot_general(left, right, dims, preferred_element_type=F32)


def attend_fwd(q_proj, own_kv, other_kv, gain, cosine, sine, q_codes, k_codes):
    rows = q_proj.shape[0]
    half = rows // 2
    keys_n = 2 * rows

    def kernel(
        q_ref, own_ref, other_ref, gain_ref, cos_ref, sin_ref, qc_ref, kc_ref,
        mix_ref, q_low_ref, total_ref, bias_ref,
    ):
        @pl.when(pl.program_id(0) == 0)
        def _():
            fill_bias(qc_ref, kc_ref, bias_ref)

        heads = []
        for g in range(2):
            values = q_ref[:, g * DH : (g + 1) * DH]
            normed = values * head_factor(values) * gain_ref[...]
            low = turn(normed, cos_ref[...], sin_ref[...]).astype(BF)
            q_low_ref[:, g * DH : (g + 1) * DH] = low
            heads.append(low)
        keys = interleave(own_ref[0], other_ref[0])
        values_t = interleave(own_ref[1], other_ref[1]).T
        for part in range(2):
            span = slice(part * half, (part + 1) * half)
            count = keys_n if part else rows
            queries = jnp.concatenate([heads[0][span], heads[1][span]], axis=0)
            bias = bias_ref[:count, span]
            scores = dot32(keys[:count], queries, NT) * (SCALE * LOG2E) + jnp.concatenate(
                [bias, bias], axis=1
            )
            row_max = jnp.max(scores, axis=0, keepdims=True)
            weights = jnp.exp2(scores - row_max)
            row_total = jnp.sum(weights, axis=0, keepdims=True)
            mix_t = dot32(values_t[:, :count], weights.astype(BF), NN) / row_total
            mix = mix_t.T.astype(BF)
            mix_ref[span, :DH] = mix[:half]
            mix_ref[span, DH:] = mix[half:]
            total_ref[0, part : part + 1, :] = row_max + jnp.log2(row_total)

    whole = lambda shape: pl.BlockSpec(shape, lambda h: (0, 0))
    pair = pl.BlockSpec((2, rows, DH), lambda h: (0, 0, h))
    wide = pl.BlockSpec((rows, 2 * DH), lambda h: (0, h))
    return pl.pallas_call(
        kernel,
        grid=(HK,),
        in_specs=[
            wide, pair, pair, whole((1, DH)), whole((rows, DH)), whole((rows, DH)),
            whole((2, rows)), whole((keys_n, 2)),
        ],
        out_specs=[wide, wide, pl.BlockSpec((1, 2, rows), lambda h: (h, 0, 0))],
        out_shape=[
            jax.ShapeDtypeStruct((rows, HQ * DH), BF),
            jax.ShapeDtypeStruct((rows, HQ * DH), BF),
            jax.ShapeDtypeStruct((HK, 2, rows), F32),
        ],
        scratch_shapes=[pltpu.VMEM((keys_n, rows), F32)],
        compiler_params=pltpu.CompilerParams(vmem_limit_bytes=48 * 2**20),
        cost_estimate=pl.CostEstimate(
            flops=HK * 2 * 2 * rows * 3 * rows * DH,
            bytes_accessed=16 * 2**20,
            transcendentals=HK * rows * 3 * rows,
        ),
        name="attend_fwd",
    )(q_proj, own_kv, other_kv, gain, cosine, sine, q_codes, k_codes)


def attend_bwd(
    q_proj, q_low, own_kv, other_kv, grad_mix, totals, gain, cosine, sine, q_codes, k_codes
):
    rows = q_proj.shape[0]
    half = rows // 2
    keys_n = 2 * rows

    def kernel(
        q_ref, q_low_ref, own_ref, other_ref, grad_ref, total_ref, gain_ref, cos_ref, sin_ref,
        qc_ref, kc_ref, grad_q_ref, grad_own_ref, grad_other_ref, gain_out, bias_ref,
    ):
        @pl.when(pl.program_id(0) == 0)
        def _():
            fill_bias(qc_ref, kc_ref, bias_ref)
            gain_out[...] = jnp.zeros_like(gain_out)

        keys = interleave(own_ref[0], other_ref[0])
        keys_t = keys.T
        values = interleave(own_ref[1], other_ref[1])
        parts_q, parts_k, parts_v = [], [], []
        for part in range(2):
            span = slice(part * half, (part + 1) * half)
            count = keys_n if part else rows
            queries = jnp.concatenate([q_low_ref[span, :DH], q_low_ref[span, DH:]], axis=0)
            grads = jnp.concatenate([grad_ref[span, :DH], grad_ref[span, DH:]], axis=0)
            bias = bias_ref[:count, span]
            scores = dot32(keys[:count], queries, NT) * (SCALE * LOG2E) + jnp.concatenate(
                [bias, bias], axis=1
            )
            probs = jnp.exp2(scores - total_ref[0, part : part + 1, :])
            grad_probs = dot32(values[:count], grads, NT)
            product = probs * grad_probs
            center = jnp.sum(product, axis=0, keepdims=True)
            grad_scores = (product - probs * center).astype(BF)
            parts_v.append(dot32(probs.astype(BF), grads, NN))
            parts_k.append(dot32(grad_scores, queries, NN) * SCALE)
            parts_q.append(dot32(keys_t[:, :count], grad_scores, NN).T * SCALE)
        for slot, parts in ((0, parts_k), (1, parts_v)):
            low_part, high_part = parts
            both = high_part[:rows] + low_part
            grad_own_ref[slot, :half] = both[:half]
            grad_other_ref[slot, :half] = both[half:].astype(BF)
            grad_own_ref[slot, half:] = high_part[rows : rows + half]
            grad_other_ref[slot, half:] = high_part[rows + half :].astype(BF)
        gain_total = gain_out[...]
        for g in range(2):
            grad_q = jnp.concatenate(
                [parts_q[0][g * half : (g + 1) * half], parts_q[1][g * half : (g + 1) * half]],
                axis=0,
            )
            grad_qn = turn(grad_q, cos_ref[...], -sin_ref[...])
            gain_grad, grad_qp = head_back(
                q_ref[:, g * DH : (g + 1) * DH], gain_ref[...], grad_qn
            )
            gain_total += gain_grad
            grad_q_ref[:, g * DH : (g + 1) * DH] = grad_qp.astype(BF)
        gain_out[...] = gain_total

    whole = lambda shape: pl.BlockSpec(shape, lambda h: (0, 0))
    pair = pl.BlockSpec((2, rows, DH), lambda h: (0, 0, h))
    wide = pl.BlockSpec((rows, 2 * DH), lambda h: (0, h))
    return pl.pallas_call(
        kernel,
        grid=(HK,),
        in_specs=[
            wide, wide, pair, pair, wide, pl.BlockSpec((1, 2, rows), lambda h: (h, 0, 0)),
            whole((1, DH)), whole((rows, DH)), whole((rows, DH)),
            whole((2, rows)), whole((keys_n, 2)),
        ],
        out_specs=[wide, pair, pair, whole((1, DH))],
        out_shape=[
            jax.ShapeDtypeStruct((rows, HQ * DH), BF),
            jax.ShapeDtypeStruct((2, rows, HK * DH), F32),
            jax.ShapeDtypeStruct((2, rows, HK * DH), BF),
            jax.ShapeDtypeStruct((1, DH), F32),
        ],
        scratch_shapes=[pltpu.VMEM((keys_n, rows), F32)],
        compiler_params=pltpu.CompilerParams(vmem_limit_bytes=56 * 2**20),
        cost_estimate=pl.CostEstimate(
            flops=HK * 5 * 2 * rows * 3 * rows * DH,
            bytes_accessed=24 * 2**20,
            transcendentals=HK * rows * 3 * rows,
        ),
        name="attend_bwd",
    )(q_proj, q_low, own_kv, other_kv, grad_mix, totals, gain, cosine, sine, q_codes, k_codes)


def mm(left, right, dims):
    return jnp.einsum(dims, left, right, preferred_element_type=F32)


def chip_local(
    dp_size, ctx_size,
    tokens, segments, positions, attn_gain, w_query, w_key, w_value, w_out, qk_gain, mlp_gain,
    w_gate, w_up, w_down, cotangent,
):
    place = Place(dp_size, ctx_size)
    _, stretch, _ = tokens.shape
    rows = 2 * stretch
    spread = lambda gain: jnp.broadcast_to(gain[:, None], (gain.shape[0], 128))

    z_kv = gather_z(place, jnp.concatenate([w_key, w_value, spread(attn_gain)], axis=1))
    z_q = gather_z(place, w_query)
    seq_tokens = to_sequences(place, after(tokens, z_kv, z_q))
    seq_positions = to_sequences(place, positions)
    other_segments = place.swap(segments, "c")
    z_out = gather_z(place, after(w_out, seq_tokens))
    z_gate = gather_z(place, after(w_gate, z_out))
    z_up = gather_z(place, after(jnp.concatenate([w_up, spread(mlp_gain)], axis=1), z_out))
    seq_cotangent = to_sequences(place, after(cotangent, z_gate, z_up))
    z_down = gather_z(place, after(w_down, seq_cotangent))

    four_kv = gather_rest(place, z_kv, "y", "x")
    four_q = gather_rest(place, z_q, "x", "y")
    four_out = gather_rest(place, after(z_out, four_q[1]), "x", "y")
    four_up = gather_rest(place, after(z_up, four_kv[1]), "y", "x")
    four_gate = gather_rest(place, after(z_gate, four_out[1]), "x", "y")
    four_down = gather_rest(place, after(z_down, four_up[1]), "y", "x")
    kv_full, g_attn = assemble(place, four_kv, "x", (2 * HK * DH, 128))
    (q_full,) = assemble(place, four_q, "y", (HQ * DH,))
    (out_full,) = assemble(place, four_out, "y", (HQ * DH,))
    up_full, g_mlp = assemble(place, four_up, "x", (w_up.shape[1], 128))
    (gate_full,) = assemble(place, four_gate, "y", (w_gate.shape[1],))
    (down_full,) = assemble(place, four_down, "x", (w_down.shape[1],))
    g_attn = g_attn[:, 0].astype(F32)
    g_mlp = g_mlp[:, 0].astype(F32)

    segment_rows = jnp.where(place.z // 2 == place.c, segments, other_segments)
    segment_row = pick(segment_rows, place.z % 2, 0)
    within = jnp.arange(stretch, dtype=jnp.int32)
    near = jnp.where(place.c == 0, 0, 1) * stretch + within
    far = jnp.where(place.c == 0, 3, 2) * stretch + within
    other_near = jnp.where(place.c == 0, 1, 0) * stretch + within
    other_far = jnp.where(place.c == 0, 2, 3) * stretch + within
    q_places = jnp.concatenate([near, far])
    k_places = jnp.concatenate([near, other_near, far, other_far])
    q_codes = jnp.stack([q_places, segment_row[q_places]])
    k_codes = jnp.stack([k_places, segment_row[k_places]], axis=1)
    inv_freq = rope_base ** (-2.0 * jnp.arange(DH // 2, dtype=F32) / DH)
    angles = seq_positions.reshape(rows).astype(F32)[:, None] * inv_freq
    cosine, sine = jnp.cos(angles), jnp.sin(angles)
    cosine = jnp.concatenate([cosine, cosine], axis=1)
    sine = jnp.concatenate([-sine, sine], axis=1)
    gains_qk = qk_gain.astype(F32)
    q_gain, k_gain = gains_qk[0:1], gains_qk[1:2]

    resid_in = seq_tokens.reshape(rows, D).astype(F32)
    normed_f, factor_in = norm_rows(resid_in, g_attn)
    normed = normed_f.astype(BF)
    kv_proj = mm(normed, kv_full, "td,dh->th")
    own_kv = prepare_kv(kv_proj, k_gain, cosine, sine)
    other_kv = place.swap(own_kv, "c")
    q_proj = mm(normed, q_full, "td,dh->th")
    attn_mix, q_low, totals = attend_fwd(
        q_proj, own_kv, other_kv, q_gain, cosine, sine, q_codes, k_codes
    )
    hidden_in = resid_in + mm(attn_mix, out_full, "th,dh->td")
    normed_mlp_f, factor_mlp = norm_rows(hidden_in, g_mlp)
    normed_mlp = normed_mlp_f.astype(BF)
    gated = mm(normed_mlp, gate_full, "td,df->tf")
    upward = mm(normed_mlp, up_full, "td,df->tf")
    sigmoid_gate = jax.nn.sigmoid(gated)
    silu_gate = gated * sigmoid_gate
    inner = (silu_gate * upward).astype(BF)
    result = (hidden_in + mm(inner, down_full, "tf,df->td")).astype(BF)
    layer_out = from_sequences(place, result.reshape(2, stretch, D))

    grad_out = seq_cotangent.reshape(rows, D)
    d_down = reduce_rows(place, mm(grad_out, inner, "td,tf->df").astype(BF), "x")
    grad_inner = mm(grad_out, down_full, "td,df->tf")
    grad_gate = (grad_inner * upward * sigmoid_gate * (1.0 + gated * (1.0 - sigmoid_gate))).astype(BF)
    grad_up = (grad_inner * silu_gate).astype(BF)
    d_gate = reduce_rows(place, mm(normed_mlp, grad_gate, "td,tf->df").astype(BF), "y")
    d_up = reduce_rows(place, mm(normed_mlp, grad_up, "td,tf->df").astype(BF), "x")
    grad_normed_mlp = mm(grad_gate, gate_full, "tf,df->td") + mm(grad_up, up_full, "tf,df->td")
    mlp_gain_part, grad_resid_mlp = norm_back(hidden_in, factor_mlp, g_mlp, grad_normed_mlp)
    grad_hidden = grad_out.astype(F32) + grad_resid_mlp

    grad_attn = grad_hidden.astype(BF)
    grad_mix = mm(grad_attn, out_full, "td,dh->th").astype(BF)
    d_out = reduce_rows(place, mm(grad_attn, attn_mix, "td,th->dh").astype(BF), "y")
    grad_q_low, own_grad, other_grad, q_gain_part = attend_bwd(
        q_proj, q_low, own_kv, other_kv, grad_mix, totals, q_gain, cosine, sine, q_codes, k_codes
    )
    received = place.swap(other_grad, "c")
    grad_kv_low, k_gain_part = finish_kv(kv_proj, own_grad, received, k_gain, cosine, sine)
    grad_kv_low = jnp.concatenate([grad_kv_low[0], grad_kv_low[1]], axis=1)
    d_query = reduce_rows(place, mm(normed, grad_q_low, "td,th->dh").astype(BF), "y")
    d_kv = reduce_rows(place, mm(normed, grad_kv_low, "td,th->dh").astype(BF), "x")
    grad_normed = mm(grad_q_low, q_full, "th,dh->td") + mm(grad_kv_low, kv_full, "th,dh->td")
    attn_gain_part, grad_resid_attn = norm_back(resid_in, factor_in, g_attn, grad_normed)
    d_seq = (grad_hidden + grad_resid_attn).astype(BF)
    d_tokens = from_sequences(place, d_seq.reshape(2, stretch, D)).astype(F32)

    small = jnp.concatenate(
        [attn_gain_part, mlp_gain_part, q_gain_part.reshape(DH), k_gain_part.reshape(DH)]
    )
    small = jnp.sum(lax.all_gather(small, AXES, axis=0, tiled=False), axis=0)
    flat = lax.axis_index("dp") * ctx_size + lax.axis_index("ctx")
    own = D // place.count
    d_attn_gain = lax.dynamic_slice_in_dim(small, flat * own, own)
    d_mlp_gain = lax.dynamic_slice_in_dim(small, D + flat * own, own)
    d_qk_gain = small[2 * D :].reshape(2, DH)
    return (
        layer_out, d_tokens, d_attn_gain, d_query, d_kv[:, : HK * DH], d_kv[:, HK * DH :], d_out,
        d_qk_gain, d_mlp_gain, d_gate, d_up, d_down,
    )


def solution(mesh):
    in_specs = (
        P("dp", "ctx", None),
        P("dp", None),
        P("dp", "ctx"),
        P(("dp", "ctx")),
        P(("dp", "ctx"), None),
        P(("dp", "ctx"), None),
        P(("dp", "ctx"), None),
        P(("dp", "ctx"), None),
        P(),
        P(("dp", "ctx")),
        P(("dp", "ctx"), None),
        P(("dp", "ctx"), None),
        P(("dp", "ctx"), None),
        P("dp", "ctx", None),
    )
    out_specs = (
        P("dp", "ctx", None),
        P("dp", "ctx", None),
        P(("dp", "ctx")),
        P(("dp", "ctx"), None),
        P(("dp", "ctx"), None),
        P(("dp", "ctx"), None),
        P(("dp", "ctx"), None),
        P(),
        P(("dp", "ctx")),
        P(("dp", "ctx"), None),
        P(("dp", "ctx"), None),
        P(("dp", "ctx"), None),
    )
    dp_size, ctx_size = mesh.shape["dp"], mesh.shape["ctx"]
    body = local
    if dp_size == 8 and ctx_size == 4:
        body = functools.partial(chip_local, dp_size, ctx_size)
    return jax.shard_map(body, mesh=mesh, in_specs=in_specs, out_specs=out_specs, check_vma=False)
```

```python
import functools
import math

import jax
import jax.numpy as jnp
from jax import lax
from jax.experimental import pallas as pl
from jax.experimental.pallas import tpu as pltpu
from jax.sharding import PartitionSpec as P

D = 1024
HQ = 16
HK = 8
DH = 128


norm_eps = 1e-06
rope_base = 1000000.0


def norm_rows(values, gain):
    factor = lax.rsqrt(jnp.mean(values * values, axis=-1, keepdims=True) + norm_eps)
    return (values * factor * gain, factor)


def norm_back(values, factor, gain, upstream):
    weighted = upstream * gain
    lead_axes = tuple(range(values.ndim - 1))
    gain_grad = jnp.sum(upstream * values * factor, axis=lead_axes)
    inner_mean = jnp.mean(weighted * values, axis=-1, keepdims=True)
    return (gain_grad, factor * weighted - values * factor * factor * factor * inner_mean)


def rotate(values, positions, sign):
    half_dim = values.shape[-1] // 2
    inv_freq = rope_base ** (-2.0 * jnp.arange(half_dim, dtype=jnp.float32) / values.shape[-1])
    angles = positions.astype(jnp.float32)[:, None, None] * inv_freq
    cosine = jnp.cos(angles)
    sine = sign * jnp.sin(angles)
    first_half = values[..., :half_dim]
    second_half = values[..., half_dim:]
    return jnp.concatenate(
        [first_half * cosine - second_half * sine, second_half * cosine + first_half * sine],
        axis=-1,
    )


def visibility(segment_row, q_first, span_len):
    key_places = jnp.arange(segment_row.shape[0], dtype=jnp.int32)
    query_places = q_first + jnp.arange(span_len, dtype=jnp.int32)
    query_segs = lax.dynamic_slice_in_dim(segment_row, q_first, span_len)
    return (query_segs[:, None] == segment_row[None, :]) & (
        key_places[None, :] <= query_places[:, None]
    )


def masked_scores(grouped, keys, visible):
    scores = jnp.einsum(
        "qhgd,khd->hgqk", grouped, keys, preferred_element_type=jnp.float32
    ) * DH ** (-0.5)
    return jnp.where(visible, scores, -1e30)


def local(
    tokens,
    segments,
    positions,
    attn_gain,
    w_query,
    w_key,
    w_value,
    w_out,
    qk_gain,
    mlp_gain,
    w_gate,
    w_up,
    w_down,
    cotangent,
):
    seq_count, span_len, _ = tokens.shape
    row_count = seq_count * span_len
    heads_per = HQ // HK
    q_first = lax.axis_index("ctx") * span_len
    pos_flat = positions.reshape(row_count)
    g_attn, wq_full, wk_full, wv_full, wo_full = (
        lax.all_gather(attn_gain, ("dp", "ctx"), axis=0, tiled=True),
        lax.all_gather(w_query, ("dp", "ctx"), axis=0, tiled=True),
        lax.all_gather(w_key, ("dp", "ctx"), axis=0, tiled=True),
        lax.all_gather(w_value, ("dp", "ctx"), axis=0, tiled=True),
        lax.all_gather(w_out, ("dp", "ctx"), axis=0, tiled=True),
    )
    resid_in = tokens.reshape(row_count, D).astype(jnp.float32)
    normed_f, factor_in = norm_rows(resid_in, g_attn.astype(jnp.float32))
    normed = normed_f.astype(jnp.bfloat16)
    q_proj = jnp.dot(normed, wq_full, preferred_element_type=jnp.float32).reshape(row_count, HQ, DH)
    k_proj = jnp.dot(normed, wk_full, preferred_element_type=jnp.float32).reshape(row_count, HK, DH)
    v_low = (
        jnp.dot(normed, wv_full, preferred_element_type=jnp.float32)
        .astype(jnp.bfloat16)
        .reshape(seq_count, span_len, HK, DH)
    )
    gains_qk = qk_gain.astype(jnp.float32)
    q_norm, factor_q = norm_rows(q_proj, gains_qk[0])
    k_norm, factor_k = norm_rows(k_proj, gains_qk[1])
    q_low = rotate(q_norm, pos_flat, 1.0).astype(jnp.bfloat16).reshape(seq_count, span_len, HQ, DH)
    k_low = rotate(k_norm, pos_flat, 1.0).astype(jnp.bfloat16).reshape(seq_count, span_len, HK, DH)
    keys_all, values_all = (
        lax.all_gather(k_low, "ctx", axis=1, tiled=True),
        lax.all_gather(v_low, "ctx", axis=1, tiled=True),
    )

    def attend_forward(group_item):
        queries, keys, values, segment_row = group_item
        visible = visibility(segment_row, q_first, span_len)
        grouped = queries.reshape(span_len, HK, heads_per, DH)
        scores = masked_scores(grouped, keys, visible)
        row_max = jnp.max(scores, axis=-1, keepdims=True)
        weights = jnp.exp(scores - row_max)
        row_total = jnp.sum(weights, axis=-1, keepdims=True)
        prob_low = (weights / row_total).astype(jnp.bfloat16)
        attn_mix = jnp.einsum(
            "hgqk,khd->qhgd", prob_low, values, preferred_element_type=jnp.float32
        )
        return (
            attn_mix.reshape(span_len, HQ * DH).astype(jnp.bfloat16),
            row_max + jnp.log(row_total),
        )

    attn_mix, log_total = lax.map(attend_forward, (q_low, keys_all, values_all, segments))
    attn_mix = attn_mix.reshape(row_count, HQ * DH)
    hidden_in = resid_in + jnp.einsum(
        "th,dh->td", attn_mix, wo_full, preferred_element_type=jnp.float32
    )
    g_mlp, wg_full, wu_full, wd_full = (
        lax.all_gather(mlp_gain, ("dp", "ctx"), axis=0, tiled=True),
        lax.all_gather(w_gate, ("dp", "ctx"), axis=0, tiled=True),
        lax.all_gather(w_up, ("dp", "ctx"), axis=0, tiled=True),
        lax.all_gather(w_down, ("dp", "ctx"), axis=0, tiled=True),
    )
    normed_mlp_f, factor_mlp = norm_rows(hidden_in, g_mlp.astype(jnp.float32))
    normed_mlp = normed_mlp_f.astype(jnp.bfloat16)
    gated = jnp.dot(normed_mlp, wg_full, preferred_element_type=jnp.float32)
    upward = jnp.dot(normed_mlp, wu_full, preferred_element_type=jnp.float32)
    sigmoid_gate = jax.nn.sigmoid(gated)
    silu_gate = gated * sigmoid_gate
    inner = (silu_gate * upward).astype(jnp.bfloat16)
    result = hidden_in + jnp.einsum("tf,df->td", inner, wd_full, preferred_element_type=jnp.float32)
    layer_out = result.astype(jnp.bfloat16).reshape(seq_count, span_len, D)
    g_mlp, wg_full, wu_full, wd_full = (
        lax.all_gather(mlp_gain, ("dp", "ctx"), axis=0, tiled=True),
        lax.all_gather(w_gate, ("dp", "ctx"), axis=0, tiled=True),
        lax.all_gather(w_up, ("dp", "ctx"), axis=0, tiled=True),
        lax.all_gather(w_down, ("dp", "ctx"), axis=0, tiled=True),
    )
    grad_out = cotangent.reshape(row_count, D)
    grad_inner = jnp.dot(grad_out, wd_full, preferred_element_type=jnp.float32)
    grad_gate = (grad_inner * upward * sigmoid_gate * (1.0 + gated * (1.0 - sigmoid_gate))).astype(
        jnp.bfloat16
    )
    grad_up = (grad_inner * silu_gate).astype(jnp.bfloat16)
    grad_normed_mlp = jnp.einsum(
        "tf,df->td", grad_gate, wg_full, preferred_element_type=jnp.float32
    )
    grad_normed_mlp = grad_normed_mlp + jnp.einsum(
        "tf,df->td", grad_up, wu_full, preferred_element_type=jnp.float32
    )
    mlp_gain_part, grad_resid_mlp = norm_back(
        hidden_in, factor_mlp, g_mlp.astype(jnp.float32), grad_normed_mlp
    )
    d_w_down = jnp.einsum("td,tf->df", grad_out, inner, preferred_element_type=jnp.float32)
    d_w_gate = jnp.einsum("td,tf->df", normed_mlp, grad_gate, preferred_element_type=jnp.float32)
    d_w_up = jnp.einsum("td,tf->df", normed_mlp, grad_up, preferred_element_type=jnp.float32)
    d_mlp_gain, d_w_gate, d_w_up, d_w_down = (
        lax.psum_scatter(mlp_gain_part, ("dp", "ctx"), scatter_dimension=0, tiled=True),
        lax.psum_scatter(d_w_gate, ("dp", "ctx"), scatter_dimension=0, tiled=True),
        lax.psum_scatter(d_w_up, ("dp", "ctx"), scatter_dimension=0, tiled=True),
        lax.psum_scatter(d_w_down, ("dp", "ctx"), scatter_dimension=0, tiled=True),
    )
    grad_hidden = grad_out.astype(jnp.float32) + grad_resid_mlp
    g_attn, wq_full, wk_full, wv_full, wo_full = (
        lax.all_gather(attn_gain, ("dp", "ctx"), axis=0, tiled=True),
        lax.all_gather(w_query, ("dp", "ctx"), axis=0, tiled=True),
        lax.all_gather(w_key, ("dp", "ctx"), axis=0, tiled=True),
        lax.all_gather(w_value, ("dp", "ctx"), axis=0, tiled=True),
        lax.all_gather(w_out, ("dp", "ctx"), axis=0, tiled=True),
    )
    grad_attn = grad_hidden.astype(jnp.bfloat16)
    grad_mix = jnp.einsum(
        "td,dh->th", grad_attn, wo_full, preferred_element_type=jnp.float32
    ).astype(jnp.bfloat16)
    grad_mix = grad_mix.reshape(seq_count, span_len, HQ, DH)

    def attend_backward(group_item):
        queries, keys, values, grad_rows, log_rows, segment_row = group_item
        visible = visibility(segment_row, q_first, span_len)
        grouped = queries.reshape(span_len, HK, heads_per, DH)
        scores = masked_scores(grouped, keys, visible)
        probs = jnp.exp(scores - log_rows)
        grad_group = grad_rows.reshape(span_len, HK, heads_per, DH)
        grad_probs = jnp.einsum(
            "qhgd,khd->hgqk", grad_group, values, preferred_element_type=jnp.float32
        )
        center = jnp.sum(probs * grad_probs, axis=-1, keepdims=True)
        grad_scores = (probs * (grad_probs - center)).astype(jnp.bfloat16)
        grad_q = jnp.einsum(
            "hgqk,khd->qhgd", grad_scores, keys, preferred_element_type=jnp.float32
        ) * DH ** (-0.5)
        grad_k = jnp.einsum(
            "hgqk,qhgd->khd", grad_scores, grouped, preferred_element_type=jnp.float32
        ) * DH ** (-0.5)
        grad_v = jnp.einsum(
            "hgqk,qhgd->khd",
            probs.astype(jnp.bfloat16),
            grad_group,
            preferred_element_type=jnp.float32,
        )
        return (grad_q.reshape(span_len, HQ, DH), grad_k, grad_v)

    grad_q, grad_k_all, grad_v_all = lax.map(
        attend_backward, (q_low, keys_all, values_all, grad_mix, log_total, segments)
    )
    grad_k, grad_v = (
        lax.psum_scatter(
            grad_k_all.astype(jnp.bfloat16), "ctx", scatter_dimension=1, tiled=True
        ).astype(jnp.float32),
        lax.psum_scatter(
            grad_v_all.astype(jnp.bfloat16), "ctx", scatter_dimension=1, tiled=True
        ).astype(jnp.float32),
    )
    grad_qn = rotate(grad_q.reshape(row_count, HQ, DH), pos_flat, -1.0)
    grad_kn = rotate(grad_k.reshape(row_count, HK, DH), pos_flat, -1.0)
    q_gain_part, grad_qp = norm_back(q_proj, factor_q, gains_qk[0], grad_qn)
    k_gain_part, grad_kp = norm_back(k_proj, factor_k, gains_qk[1], grad_kn)
    grad_q_low = grad_qp.reshape(row_count, HQ * DH).astype(jnp.bfloat16)
    grad_k_low = grad_kp.reshape(row_count, HK * DH).astype(jnp.bfloat16)
    grad_v_low = grad_v.reshape(row_count, HK * DH).astype(jnp.bfloat16)
    grad_normed = jnp.einsum("th,dh->td", grad_q_low, wq_full, preferred_element_type=jnp.float32)
    grad_normed = grad_normed + jnp.einsum(
        "th,dh->td", grad_k_low, wk_full, preferred_element_type=jnp.float32
    )
    grad_normed = grad_normed + jnp.einsum(
        "th,dh->td", grad_v_low, wv_full, preferred_element_type=jnp.float32
    )
    attn_gain_part, grad_resid_attn = norm_back(
        resid_in, factor_in, g_attn.astype(jnp.float32), grad_normed
    )
    d_qk_gain = lax.psum(jnp.stack([q_gain_part, k_gain_part]), ("dp", "ctx"))
    d_w_out = jnp.einsum("td,th->dh", grad_attn, attn_mix, preferred_element_type=jnp.float32)
    d_w_query = jnp.einsum("td,th->dh", normed, grad_q_low, preferred_element_type=jnp.float32)
    d_w_key = jnp.einsum("td,th->dh", normed, grad_k_low, preferred_element_type=jnp.float32)
    d_w_value = jnp.einsum("td,th->dh", normed, grad_v_low, preferred_element_type=jnp.float32)
    d_attn_gain, d_w_query, d_w_key, d_w_value, d_w_out = (
        lax.psum_scatter(attn_gain_part, ("dp", "ctx"), scatter_dimension=0, tiled=True),
        lax.psum_scatter(d_w_query, ("dp", "ctx"), scatter_dimension=0, tiled=True),
        lax.psum_scatter(d_w_key, ("dp", "ctx"), scatter_dimension=0, tiled=True),
        lax.psum_scatter(d_w_value, ("dp", "ctx"), scatter_dimension=0, tiled=True),
        lax.psum_scatter(d_w_out, ("dp", "ctx"), scatter_dimension=0, tiled=True),
    )
    d_tokens = (grad_hidden + grad_resid_attn).reshape(seq_count, span_len, D)
    return (
        layer_out,
        d_tokens,
        d_attn_gain,
        d_w_query,
        d_w_key,
        d_w_value,
        d_w_out,
        d_qk_gain,
        d_mlp_gain,
        d_w_gate,
        d_w_up,
        d_w_down,
    )


AXES = ("dp", "ctx")
SCALE = DH ** (-0.5)
LOG2E = math.log2(math.e)
NEG = -1e30
BF = jnp.bfloat16
F32 = jnp.float32


class Place:
    def __init__(self, dp_size, ctx_size):
        self.count = dp_size * ctx_size
        self.z_size = ctx_size
        dp = lax.axis_index("dp")
        self.z = lax.axis_index("ctx")
        self.c = dp % 2
        self.x = (dp // 2) % 2
        self.y = dp // 4

    def split(self, flat):
        z, dp = flat % self.z_size, flat // self.z_size
        return dp // 4, (dp // 2) % 2, dp % 2, z

    def join(self, y, x, c, z):
        return ((y * 2 + x) * 2 + c) * self.z_size + z

    def move(self, values, target):
        perm = []
        for flat in range(self.count):
            perm.append((flat, self.join(*target(*self.split(flat)))))
        return lax.ppermute(values, AXES, perm)

    def swap(self, values, axis):
        return self.move(
            values,
            lambda y, x, c, z: (
                1 - y if axis == "y" else y,
                1 - x if axis == "x" else x,
                1 - c if axis == "c" else c,
                z,
            ),
        )

    def shift(self, values, step):
        return self.move(values, lambda y, x, c, z: (y, x, c, (z + step) % self.z_size))


def arrived(earlier):
    first = earlier[(0,) * earlier.ndim]
    return (first != first).astype(jnp.int32)


def all_arrived(*earlier):
    return sum(arrived(one) for one in earlier).reshape(1)


STRETCHES = ((0, 3), (1, 2))
CORE_OF = (0, 1, 1, 0)
RANK_OF = (0, 0, 1, 1)


def rank_here(place):
    return jnp.asarray(RANK_OF, jnp.int32)[place.z]


def to_sequences(place, values, late=0):
    parts = []
    for m in range(2):
        chosen = pick(values, (rank_here(place) + m) % 2 + 2 * late, 0)
        parts.append(
            place.move(
                chosen, lambda y, x, c, z: (y, x, CORE_OF[z], 2 * c + (RANK_OF[z] + m) % 2)
            )
        )
    first, second = parts
    even = place.z % 2 == 0
    return jnp.concatenate(
        [jnp.where(even, first, second), jnp.where(even, second, first)], axis=0
    )


def from_sequences(place, values, late=0):
    parts = []
    for m in range(2):
        chosen = pick(values, (m + place.z) % 2 + 2 * late, 0)
        parts.append(
            place.move(
                chosen,
                lambda y, x, c, z: (y, x, z // 2, STRETCHES[c][(m + z) % 2]),
            )
        )
    first, second = parts
    even = rank_here(place) == 0
    return jnp.stack([jnp.where(even, first, second), jnp.where(even, second, first)])


def gather_z(place, shards, late=0):
    widths = [shard.shape[1] for shard in shards]
    shard = jnp.concatenate(shards, axis=1)
    shard = jnp.where(late == 0, shard, jnp.zeros_like(shard))
    pieces = [shard]
    for _ in range(1, place.z_size):
        pieces.append(place.shift(pieces[-1], 1))
    start, stacks = 0, []
    for width in widths:
        stacks.append(jnp.stack([piece[:, start : start + width] for piece in pieces]))
        start += width
    return stacks, pieces


class Lanes:
    def __init__(self):
        self.last = {}

    def late(self, axis):
        return arrived(self.last[axis]) if axis in self.last else jnp.int32(0)

    def swap(self, place, values, axis):
        self.last[axis] = place.swap(values, axis)
        return self.last[axis]


def gather_pair(place, lanes, one, two, *earlier):
    if earlier:
        one = jnp.where(arrived(earlier[0]) == 0, one, jnp.zeros_like(one))
        two = jnp.where(arrived(earlier[1]) == 0, two, jnp.zeros_like(two))
    one = jnp.stack([one, lanes.swap(place, one, "x")])
    two = jnp.stack([two, lanes.swap(place, two, "y")])
    one_far = lanes.swap(place, one, "y")
    two_far = lanes.swap(place, two, "x")
    return tuple(
        (near, far, place.swap(near, "c"), place.swap(far, "c"))
        for near, far in ((one, one_far), (two, two_far))
    )


def assemble(place, quarters, second_axis, widths):
    z_size, rows, total = place.z_size, quarters[0].shape[2], quarters[0].shape[3]
    first_is_x = second_axis == "y"
    here = jnp.stack(
        [place.x if first_is_x else place.y, place.y if first_is_x else place.x, place.c, place.z]
    ).astype(jnp.int32)

    def kernel(here_ref, near, far, near_core, far_core, *outs):
        second, core = here_ref[1], here_ref[2]
        for ref, from_second, from_core in (
            (near, 0, 0),
            (far, 1, 0),
            (near_core, 0, 1),
            (far_core, 1, 1),
        ):
            at_second = lax.rem(second + from_second, 2)
            at_core = lax.rem(core + from_core, 2)
            start = 0
            for out, width in zip(outs, widths):
                block = ref[0, 0, :, start : start + width]
                if first_is_x:
                    out[at_second, 0, at_core, 0] = block
                else:
                    out[0, at_second, at_core, 0] = block
                start += width

    def in_map(i, k, here_ref):
        return (i, k, 0, 0)

    def out_map(i, k, here_ref):
        first = lax.rem(here_ref[0] + i, 2)
        z = lax.rem(here_ref[3] + z_size - k, z_size)
        return (0, first, 0, z, 0, 0) if first_is_x else (first, 0, 0, z, 0, 0)

    def out_block(width):
        return (2, 1, 2, 1, rows, width) if first_is_x else (1, 2, 2, 1, rows, width)

    outs = pl.pallas_call(
        kernel,
        grid_spec=pltpu.PrefetchScalarGridSpec(
            num_scalar_prefetch=1,
            grid=(2, z_size),
            in_specs=[pl.BlockSpec((1, 1, rows, total), in_map)] * 4,
            out_specs=[pl.BlockSpec(out_block(width), out_map) for width in widths],
        ),
        out_shape=[
            jax.ShapeDtypeStruct((2, 2, 2, z_size, rows, width), BF) for width in widths
        ],
        compiler_params=pltpu.CompilerParams(vmem_limit_bytes=32 * 2**20),
        cost_estimate=pl.CostEstimate(
            flops=0, bytes_accessed=2 * 8 * z_size * rows * total * 2, transcendentals=0
        ),
        name="assemble",
    )(here, *quarters)
    return [out.reshape(8 * z_size * rows, out.shape[-1]) for out in outs]


def pick(values, index, axis):
    return lax.dynamic_index_in_dim(values, index, axis, keepdims=False)


def arrange(place, values, late=None):
    rows, width = values.shape
    z_size, part = place.z_size, width // place.count
    here = jnp.stack([place.c, place.x, place.y, place.z]).astype(jnp.int32)
    if late is not None:
        here = here + late

    width_z = z_size * part

    def kernel(here_ref, in_ref, out_x_ref, out_y_ref):
        for core in range(2):
            for at_x in range(2):
                for at_y in range(2):
                    c, x, y = (
                        lax.rem(here_ref[k] + at, 2) for k, at in enumerate((core, at_x, at_y))
                    )
                    start = pl.multiple_of(((y * 2 + x) * 2 + c) * width_z, width_z)
                    turned = pltpu.roll(
                        in_ref[:, pl.ds(start, width_z)].astype(F32),
                        lax.rem(z_size - here_ref[3], z_size) * part,
                        1,
                    ).astype(BF)
                    for out_ref, place_of in (
                        (out_x_ref, core * 4 + at_x * 2 + at_y),
                        (out_y_ref, core * 4 + at_y * 2 + at_x),
                    ):
                        out_ref[:, place_of * width_z : (place_of + 1) * width_z] = turned

    whole = pl.BlockSpec((rows, width), lambda i, here_ref: (0, 0))
    out_x, out_y = pl.pallas_call(
        kernel,
        grid_spec=pltpu.PrefetchScalarGridSpec(
            num_scalar_prefetch=1, grid=(1,), in_specs=[whole], out_specs=[whole, whole]
        ),
        out_shape=[jax.ShapeDtypeStruct((rows, width), BF)] * 2,
        compiler_params=pltpu.CompilerParams(vmem_limit_bytes=32 * 2**20),
        cost_estimate=pl.CostEstimate(
            flops=0, bytes_accessed=6 * rows * width, transcendentals=0
        ),
        name="arrange",
    )(here, values)
    return {"xy": out_x, "yx": out_y}


TN = (((0,), (0,)), ((), ()))


class Reduction:
    def __init__(self, place, left, right, axes):
        self.place, self.left, self.right, self.axes = place, left[axes], right, axes
        self.half = self.left.shape[1] // 2

    def product(self, start, end):
        return dot32(self.left[:, start:end], self.right, TN)

    def core(self):
        half = self.half
        sent = self.product(half, 2 * half).astype(BF)
        self.from_core = self.place.swap(sent, "c")
        return self.from_core

    def first(self):
        half = self.half
        sent = self.product(half // 2, half) + self.from_core[half // 2 :].astype(F32)
        self.from_first = self.place.swap(sent.astype(BF), self.axes[0])
        return self.from_first

    def second(self):
        quarter = self.half // 2
        total = self.product(0, quarter) + self.from_core[:quarter].astype(F32)
        total = (total + self.from_first.astype(F32)).astype(BF)
        self.kept = total[: quarter // 2]
        self.from_second = self.place.swap(total[quarter // 2 :], self.axes[1])
        return self.from_second

    def rest(self):
        return (self.kept.astype(F32) + self.from_second.astype(F32)).astype(BF)


def finish_rows(place, parts):
    rows = parts.shape[0] // place.z_size
    total = parts[:rows].astype(F32)
    for k in range(1, place.z_size):
        total = total + place.shift(parts[k * rows : (k + 1) * rows], k).astype(F32)
    return total


def sum_everywhere(place, values):
    for axis in ("c", "y", "x"):
        values = values + place.swap(values, axis)
    step = 1
    while step < place.z_size:
        values = values + place.move(values, lambda y, x, c, z: (y, x, c, z ^ step))
        step *= 2
    return values


def head_factor(values):
    return lax.rsqrt(jnp.mean(values * values, axis=-1, keepdims=True) + norm_eps)


def head_back(values, gain, upstream):
    factor = head_factor(values)
    weighted = upstream * gain
    gain_grad = jnp.sum(upstream * values * factor, axis=0, keepdims=True)
    inner_mean = jnp.mean(weighted * values, axis=-1, keepdims=True)
    return gain_grad, factor * weighted - values * factor * factor * factor * inner_mean


def turn(values, cosine, sine):
    return values * cosine + pltpu.roll(values, DH // 2, 1) * sine


def prepare_kv(kv_proj, gain, cosine, sine):
    rows = kv_proj.shape[0]

    def kernel(k_ref, v_ref, gain_ref, cos_ref, sin_ref, out_ref):
        values = k_ref[...]
        normed = values * head_factor(values) * gain_ref[...]
        out_ref[0] = turn(normed, cos_ref[...], sin_ref[...]).astype(BF)
        out_ref[1] = v_ref[...].astype(BF)

    whole = lambda shape: pl.BlockSpec(shape, lambda h: (0, 0))
    return pl.pallas_call(
        kernel,
        grid=(HK,),
        in_specs=[
            pl.BlockSpec((rows, DH), lambda h: (0, h)),
            pl.BlockSpec((rows, DH), lambda h: (0, HK + h)),
            whole((1, DH)),
            whole((rows, DH)),
            whole((rows, DH)),
        ],
        out_specs=pl.BlockSpec((2, rows, DH), lambda h: (0, 0, h)),
        out_shape=jax.ShapeDtypeStruct((2, rows, HK * DH), BF),
        cost_estimate=pl.CostEstimate(
            flops=10 * rows * HK * DH, bytes_accessed=12 * rows * HK * DH, transcendentals=0
        ),
        name="prepare_kv",
    )(kv_proj, kv_proj, gain, cosine, sine)


def finish_kv(late, kv_proj, own, received, gain, cosine, sine):
    rows = kv_proj.shape[0]

    def kernel(late_ref, k_ref, own_ref, other_ref, gain_ref, cos_ref, sin_ref, out_ref, gain_out):
        @pl.when(pl.program_id(0) == 0)
        def _():
            gain_out[...] = jnp.zeros_like(gain_out)

        grad_k = own_ref[0] + other_ref[0].astype(F32)
        grad_kn = turn(grad_k, cos_ref[...], -sin_ref[...])
        gain_grad, grad_kp = head_back(k_ref[...], gain_ref[...], grad_kn)
        gain_out[...] += gain_grad
        out_ref[0] = grad_kp.astype(BF)
        out_ref[1] = (own_ref[1] + other_ref[1].astype(F32)).astype(BF)

    whole = lambda shape: pl.BlockSpec(shape, lambda h: (0, 0))
    pair = pl.BlockSpec((2, rows, DH), lambda h: (0, 0, h))
    return pl.pallas_call(
        kernel,
        grid=(HK,),
        in_specs=[
            pl.BlockSpec(memory_space=pltpu.SMEM),
            pl.BlockSpec((rows, DH), lambda h: (0, h)),
            pair,
            pair,
            whole((1, DH)),
            whole((rows, DH)),
            whole((rows, DH)),
        ],
        out_specs=[pair, whole((1, DH))],
        out_shape=[
            jax.ShapeDtypeStruct((2, rows, HK * DH), BF),
            jax.ShapeDtypeStruct((1, DH), F32),
        ],
        cost_estimate=pl.CostEstimate(
            flops=30 * rows * HK * DH, bytes_accessed=20 * rows * HK * DH, transcendentals=0
        ),
        name="finish_kv",
    )(late, kv_proj, own, received, gain, cosine, sine)


def interleave(own, other):
    half = own.shape[0] // 2
    return jnp.concatenate([own[:half], other[:half], own[half:], other[half:]], axis=0)


def fill_bias(q_ref, k_ref, bias_ref):
    bias_ref[...] = jnp.where(
        (k_ref[:, 0:1] <= q_ref[0:1, :]) & (k_ref[:, 1:2] == q_ref[1:2, :]), 0.0, NEG
    ).astype(F32)


NT = (((1,), (1,)), ((), ()))
NN = (((1,), (0,)), ((), ()))


def dot32(left, right, dims):
    return lax.dot_general(left, right, dims, preferred_element_type=F32)


def attend_fwd(q_proj, own_kv, other_kv, gain, cosine, sine, q_codes, k_codes):
    rows = q_proj.shape[0]
    half = rows // 2
    keys_n = 2 * rows

    def kernel(
        q_ref, own_ref, other_ref, gain_ref, cos_ref, sin_ref, qc_ref, kc_ref,
        mix_ref, q_low_ref, total_ref, bias_ref,
    ):
        @pl.when(pl.program_id(0) == 0)
        def _():
            fill_bias(qc_ref, kc_ref, bias_ref)

        heads = []
        for g in range(2):
            values = q_ref[:, g * DH : (g + 1) * DH]
            normed = values * head_factor(values) * gain_ref[...]
            low = turn(normed, cos_ref[...], sin_ref[...]).astype(BF)
            q_low_ref[:, g * DH : (g + 1) * DH] = low
            heads.append(low)
        keys = interleave(own_ref[0], other_ref[0])
        values_t = interleave(own_ref[1], other_ref[1]).T
        for part in range(2):
            span = slice(part * half, (part + 1) * half)
            count = keys_n if part else rows
            queries = jnp.concatenate([heads[0][span], heads[1][span]], axis=0)
            bias = bias_ref[:count, span]
            scores = dot32(keys[:count], queries, NT) * (SCALE * LOG2E) + jnp.concatenate(
                [bias, bias], axis=1
            )
            row_max = jnp.max(scores, axis=0, keepdims=True)
            weights = jnp.exp2(scores - row_max)
            row_total = jnp.sum(weights, axis=0, keepdims=True)
            mix_t = dot32(values_t[:, :count], weights.astype(BF), NN) / row_total
            mix = mix_t.T.astype(BF)
            mix_ref[span, :DH] = mix[:half]
            mix_ref[span, DH:] = mix[half:]
            total_ref[0, part : part + 1, :] = row_max + jnp.log2(row_total)

    whole = lambda shape: pl.BlockSpec(shape, lambda h: (0, 0))
    pair = pl.BlockSpec((2, rows, DH), lambda h: (0, 0, h))
    wide = pl.BlockSpec((rows, 2 * DH), lambda h: (0, h))
    return pl.pallas_call(
        kernel,
        grid=(HK,),
        in_specs=[
            wide, pair, pair, whole((1, DH)), whole((rows, DH)), whole((rows, DH)),
            whole((2, rows)), whole((keys_n, 2)),
        ],
        out_specs=[wide, wide, pl.BlockSpec((1, 2, rows), lambda h: (h, 0, 0))],
        out_shape=[
            jax.ShapeDtypeStruct((rows, HQ * DH), BF),
            jax.ShapeDtypeStruct((rows, HQ * DH), BF),
            jax.ShapeDtypeStruct((HK, 2, rows), F32),
        ],
        scratch_shapes=[pltpu.VMEM((keys_n, rows), F32)],
        compiler_params=pltpu.CompilerParams(vmem_limit_bytes=48 * 2**20),
        cost_estimate=pl.CostEstimate(
            flops=HK * 2 * 2 * rows * 3 * rows * DH,
            bytes_accessed=16 * 2**20,
            transcendentals=HK * rows * 3 * rows,
        ),
        name="attend_fwd",
    )(q_proj, own_kv, other_kv, gain, cosine, sine, q_codes, k_codes)


def attend_bwd(
    late, q_proj, q_low, own_kv, other_kv, grad_mix, totals, gain, cosine, sine, q_codes, k_codes
):
    rows = q_proj.shape[0]
    half = rows // 2
    keys_n = 2 * rows

    def kernel(
        late_ref, q_ref, q_low_ref, own_ref, other_ref, grad_ref, total_ref, gain_ref, cos_ref, sin_ref,
        qc_ref, kc_ref, grad_q_ref, grad_own_ref, grad_other_ref, gain_out, bias_ref,
    ):
        @pl.when(pl.program_id(0) == 0)
        def _():
            fill_bias(qc_ref, kc_ref, bias_ref)
            gain_out[...] = jnp.zeros_like(gain_out)

        keys = interleave(own_ref[0], other_ref[0])
        keys_t = keys.T
        values = interleave(own_ref[1], other_ref[1])
        parts_q, parts_k, parts_v = [], [], []
        for part in range(2):
            span = slice(part * half, (part + 1) * half)
            count = keys_n if part else rows
            queries = jnp.concatenate([q_low_ref[span, :DH], q_low_ref[span, DH:]], axis=0)
            grads = jnp.concatenate([grad_ref[span, :DH], grad_ref[span, DH:]], axis=0)
            bias = bias_ref[:count, span]
            scores = dot32(keys[:count], queries, NT) * (SCALE * LOG2E) + jnp.concatenate(
                [bias, bias], axis=1
            )
            probs = jnp.exp2(scores - total_ref[0, part : part + 1, :])
            grad_probs = dot32(values[:count], grads, NT)
            product = probs * grad_probs
            center = jnp.sum(product, axis=0, keepdims=True)
            grad_scores = (product - probs * center).astype(BF)
            parts_v.append(dot32(probs.astype(BF), grads, NN))
            parts_k.append(dot32(grad_scores, queries, NN) * SCALE)
            parts_q.append(dot32(keys_t[:, :count], grad_scores, NN).T * SCALE)
        for slot, parts in ((0, parts_k), (1, parts_v)):
            low_part, high_part = parts
            both = high_part[:rows] + low_part
            grad_own_ref[slot, :half] = both[:half]
            grad_other_ref[slot, :half] = both[half:].astype(BF)
            grad_own_ref[slot, half:] = high_part[rows : rows + half]
            grad_other_ref[slot, half:] = high_part[rows + half :].astype(BF)
        gain_total = gain_out[...]
        for g in range(2):
            grad_q = jnp.concatenate(
                [parts_q[0][g * half : (g + 1) * half], parts_q[1][g * half : (g + 1) * half]],
                axis=0,
            )
            grad_qn = turn(grad_q, cos_ref[...], -sin_ref[...])
            gain_grad, grad_qp = head_back(
                q_ref[:, g * DH : (g + 1) * DH], gain_ref[...], grad_qn
            )
            gain_total += gain_grad
            grad_q_ref[:, g * DH : (g + 1) * DH] = grad_qp.astype(BF)
        gain_out[...] = gain_total

    whole = lambda shape: pl.BlockSpec(shape, lambda h: (0, 0))
    pair = pl.BlockSpec((2, rows, DH), lambda h: (0, 0, h))
    wide = pl.BlockSpec((rows, 2 * DH), lambda h: (0, h))
    return pl.pallas_call(
        kernel,
        grid=(HK,),
        in_specs=[
            pl.BlockSpec(memory_space=pltpu.SMEM),
            wide, wide, pair, pair, wide, pl.BlockSpec((1, 2, rows), lambda h: (h, 0, 0)),
            whole((1, DH)), whole((rows, DH)), whole((rows, DH)),
            whole((2, rows)), whole((keys_n, 2)),
        ],
        out_specs=[wide, pair, pair, whole((1, DH))],
        out_shape=[
            jax.ShapeDtypeStruct((rows, HQ * DH), BF),
            jax.ShapeDtypeStruct((2, rows, HK * DH), F32),
            jax.ShapeDtypeStruct((2, rows, HK * DH), BF),
            jax.ShapeDtypeStruct((1, DH), F32),
        ],
        scratch_shapes=[pltpu.VMEM((keys_n, rows), F32)],
        compiler_params=pltpu.CompilerParams(vmem_limit_bytes=56 * 2**20),
        cost_estimate=pl.CostEstimate(
            flops=HK * 5 * 2 * rows * 3 * rows * DH,
            bytes_accessed=24 * 2**20,
            transcendentals=HK * rows * 3 * rows,
        ),
        name="attend_bwd",
    )(late, q_proj, q_low, own_kv, other_kv, grad_mix, totals, gain, cosine, sine, q_codes, k_codes)


def mm(left, right, dims):
    return jnp.einsum(dims, left, right, preferred_element_type=F32)


def chip_local(
    dp_size, ctx_size,
    tokens, segments, positions, attn_gain, w_query, w_key, w_value, w_out, qk_gain, mlp_gain,
    w_gate, w_up, w_down, cotangent,
):
    place = Place(dp_size, ctx_size)
    _, stretch, _ = tokens.shape
    rows = 2 * stretch
    spread = lambda gain: jnp.broadcast_to(gain[:, None], (gain.shape[0], 128))

    lanes = Lanes()
    spread_kv = jnp.concatenate([w_key, w_value, spread(attn_gain)], axis=1)
    spread_up = jnp.concatenate([w_up, spread(mlp_gain)], axis=1)
    (z_q, z_kv), came = gather_z(place, [w_query, spread_kv])
    seq_tokens = to_sequences(place, tokens, arrived(came[-1]))
    other_segments = place.swap(segments, "c")
    four_q, four_kv = gather_pair(place, lanes, z_q, z_kv)
    seq_positions = to_sequences(place, positions, arrived(four_kv[1]))
    (z_out, z_up), came = gather_z(
        place, [w_out, spread_up], arrived(seq_tokens) + arrived(four_q[0]) + arrived(four_kv[0])
    )
    four_out, four_up = gather_pair(place, lanes, z_out, z_up, four_kv[3], four_q[3])
    (z_gate, z_down), came = gather_z(
        place, [w_gate, w_down], arrived(four_out[0]) + arrived(four_up[0])
    )
    four_gate, four_down = gather_pair(
        place, lanes, z_gate, z_down, lanes.last["x"], lanes.last["y"]
    )
    seq_cotangent = to_sequences(place, cotangent, arrived(four_gate[0]) + arrived(four_down[0]))
    kv_full, g_attn = assemble(place, four_kv, "x", (2 * HK * DH, 128))
    (q_full,) = assemble(place, four_q, "y", (HQ * DH,))
    (out_full,) = assemble(place, four_out, "y", (HQ * DH,))
    up_full, g_mlp = assemble(place, four_up, "x", (w_up.shape[1], 128))
    (gate_full,) = assemble(place, four_gate, "y", (w_gate.shape[1],))
    (down_full,) = assemble(place, four_down, "x", (w_down.shape[1],))
    g_attn = g_attn[:, 0].astype(F32)
    g_mlp = g_mlp[:, 0].astype(F32)

    segment_rows = jnp.where(place.z // 2 == place.c, segments, other_segments)
    segment_row = pick(segment_rows, place.z % 2, 0)
    within = jnp.arange(stretch, dtype=jnp.int32)
    near, far, other_near, other_far = (
        jnp.where(place.c == 0, left, right) for left, right in ((0, 1), (3, 2), (1, 0), (2, 3))
    )
    codes = [
        jnp.stack(
            [k * stretch + within, lax.dynamic_slice_in_dim(segment_row, k * stretch, stretch)]
        )
        for k in (near, other_near, far, other_far)
    ]
    q_codes = jnp.concatenate([codes[0], codes[2]], axis=1)
    k_codes = jnp.concatenate(codes, axis=1).T
    inv_freq = rope_base ** (-2.0 * jnp.arange(DH // 2, dtype=F32) / DH)
    angles = seq_positions.reshape(rows).astype(F32)[:, None] * inv_freq
    cosine, sine = jnp.cos(angles), jnp.sin(angles)
    cosine = jnp.concatenate([cosine, cosine], axis=1)
    sine = jnp.concatenate([-sine, sine], axis=1)
    gains_qk = qk_gain.astype(F32)
    q_gain, k_gain = gains_qk[0:1], gains_qk[1:2]

    resid_in = seq_tokens.reshape(rows, D).astype(F32)
    normed_f, factor_in = norm_rows(resid_in, g_attn)
    normed = normed_f.astype(BF)
    kv_proj = mm(normed, kv_full, "td,dh->th")
    own_kv = prepare_kv(kv_proj, k_gain, cosine, sine)
    other_kv = place.swap(own_kv, "c")
    q_proj = mm(normed, q_full, "td,dh->th")
    attn_mix, q_low, totals = attend_fwd(
        q_proj, own_kv, other_kv, q_gain, cosine, sine, q_codes, k_codes
    )
    hidden_in = resid_in + mm(attn_mix, out_full, "th,dh->td")
    normed_mlp_f, factor_mlp = norm_rows(hidden_in, g_mlp)
    normed_mlp = normed_mlp_f.astype(BF)
    gated = mm(normed_mlp, gate_full, "td,df->tf")
    upward = mm(normed_mlp, up_full, "td,df->tf")
    sigmoid_gate = jax.nn.sigmoid(gated)
    silu_gate = gated * sigmoid_gate
    inner = (silu_gate * upward).astype(BF)
    result = (hidden_in + mm(inner, down_full, "tf,df->td")).astype(BF)
    layer_out = from_sequences(place, result.reshape(2, stretch, D))

    grad_out = seq_cotangent.reshape(rows, D)
    middle = inner.shape[1] // 2
    by_out = arrange(place, grad_out)
    down_left = Reduction(place, by_out, inner[:, :middle], "xy")
    down_right = Reduction(place, by_out, inner[:, middle:], "yx")
    down_left.core(), down_right.core()
    grad_inner = mm(grad_out, down_full, "td,df->tf")
    grad_gate = (grad_inner * upward * sigmoid_gate * (1.0 + gated * (1.0 - sigmoid_gate))).astype(BF)
    grad_up = (grad_inner * silu_gate).astype(BF)
    by_mlp = arrange(place, normed_mlp)
    gate = Reduction(place, by_mlp, grad_gate, "yx")
    up = Reduction(place, by_mlp, grad_up, "xy")
    waits = [gate.core(), up.core(), down_left.first(), down_right.first()]
    grad_normed_mlp = mm(grad_gate, gate_full, "tf,df->td") + mm(grad_up, up_full, "tf,df->td")
    mlp_gain_part, grad_resid_mlp = norm_back(hidden_in, factor_mlp, g_mlp, grad_normed_mlp)
    grad_hidden = grad_out.astype(F32) + grad_resid_mlp

    grad_attn = grad_hidden.astype(BF)
    grad_mix = mm(grad_attn, out_full, "td,dh->th").astype(BF)
    grad_q_low, own_grad, other_grad, q_gain_part = attend_bwd(
        all_arrived(*waits),
        q_proj, q_low, own_kv, other_kv, grad_mix, totals, q_gain, cosine, sine, q_codes, k_codes,
    )
    received = place.swap(other_grad, "c")
    middle = attn_mix.shape[1] // 2
    by_attn = arrange(place, grad_attn)
    out_left = Reduction(place, by_attn, attn_mix[:, :middle], "xy")
    out_right = Reduction(place, by_attn, attn_mix[:, middle:], "yx")
    waits = [gate.first(), up.first(), out_left.core(), out_right.core()]
    grad_kv_low, k_gain_part = finish_kv(
        all_arrived(*waits), kv_proj, own_grad, received, k_gain, cosine, sine
    )
    grad_kv_low = jnp.concatenate([grad_kv_low[0], grad_kv_low[1]], axis=1)
    by_in = arrange(place, normed)
    query = Reduction(place, by_in, grad_q_low, "yx")
    kv = Reduction(place, by_in, grad_kv_low, "xy")
    starts = [query.core(), kv.core()]
    early = [gate, up, down_left, down_right]
    late = [query, kv, out_left, out_right]
    for one in early:
        one.second()
    for one in (query, kv, out_left, out_right):
        one.first()
    for one in (query, kv, out_left, out_right):
        one.second()
    d_early = finish_rows(place, jnp.concatenate([one.rest() for one in early], axis=1))
    d_late = finish_rows(place, jnp.concatenate([one.rest() for one in late], axis=1))
    ff, wide = w_gate.shape[1], HQ * DH
    d_gate, d_up, d_down = d_early[:, :ff], d_early[:, ff : 2 * ff], d_early[:, 2 * ff :]
    d_query, d_kv, d_out = d_late[:, :wide], d_late[:, wide : 2 * wide], d_late[:, 2 * wide :]
    grad_normed = mm(grad_q_low, q_full, "th,dh->td") + mm(grad_kv_low, kv_full, "th,dh->td")
    attn_gain_part, grad_resid_attn = norm_back(resid_in, factor_in, g_attn, grad_normed)
    d_seq = (grad_hidden + grad_resid_attn).astype(BF)
    d_tokens = from_sequences(place, d_seq.reshape(2, stretch, D)).astype(F32)

    small = jnp.concatenate(
        [attn_gain_part, mlp_gain_part, q_gain_part.reshape(DH), k_gain_part.reshape(DH)]
    )
    small = jnp.where(all_arrived(*starts)[0] == 0, small, 0.0)
    small = sum_everywhere(place, small.reshape(-1, 128)).reshape(-1)
    flat = lax.axis_index("dp") * ctx_size + lax.axis_index("ctx")
    own = D // place.count
    d_attn_gain = lax.dynamic_slice_in_dim(small, flat * own, own)
    d_mlp_gain = lax.dynamic_slice_in_dim(small, D + flat * own, own)
    d_qk_gain = small[2 * D :].reshape(2, DH)
    return (
        layer_out, d_tokens, d_attn_gain, d_query, d_kv[:, : HK * DH], d_kv[:, HK * DH :], d_out,
        d_qk_gain, d_mlp_gain, d_gate, d_up, d_down,
    )


def solution(mesh):
    in_specs = (
        P("dp", "ctx", None),
        P("dp", None),
        P("dp", "ctx"),
        P(("dp", "ctx")),
        P(("dp", "ctx"), None),
        P(("dp", "ctx"), None),
        P(("dp", "ctx"), None),
        P(("dp", "ctx"), None),
        P(),
        P(("dp", "ctx")),
        P(("dp", "ctx"), None),
        P(("dp", "ctx"), None),
        P(("dp", "ctx"), None),
        P("dp", "ctx", None),
    )
    out_specs = (
        P("dp", "ctx", None),
        P("dp", "ctx", None),
        P(("dp", "ctx")),
        P(("dp", "ctx"), None),
        P(("dp", "ctx"), None),
        P(("dp", "ctx"), None),
        P(("dp", "ctx"), None),
        P(),
        P(("dp", "ctx")),
        P(("dp", "ctx"), None),
        P(("dp", "ctx"), None),
        P(("dp", "ctx"), None),
    )
    dp_size, ctx_size = mesh.shape["dp"], mesh.shape["ctx"]
    body = local
    if dp_size == 8 and ctx_size == 4:
        body = functools.partial(chip_local, dp_size, ctx_size)
    return jax.shard_map(body, mesh=mesh, in_specs=in_specs, out_specs=out_specs, check_vma=False)
```

```python
import functools
import math

import jax
import jax.numpy as jnp
from jax import lax
from jax.experimental import pallas as pl
from jax.experimental.pallas import tpu as pltpu
from jax.sharding import PartitionSpec as P

D = 1024
HQ = 16
HK = 8
DH = 128


norm_eps = 1e-06
rope_base = 1000000.0


def norm_rows(values, gain):
    factor = lax.rsqrt(jnp.mean(values * values, axis=-1, keepdims=True) + norm_eps)
    return (values * factor * gain, factor)


def norm_back(values, factor, gain, upstream):
    weighted = upstream * gain
    lead_axes = tuple(range(values.ndim - 1))
    gain_grad = jnp.sum(upstream * values * factor, axis=lead_axes)
    inner_mean = jnp.mean(weighted * values, axis=-1, keepdims=True)
    return (gain_grad, factor * weighted - values * factor * factor * factor * inner_mean)


def rotate(values, positions, sign):
    half_dim = values.shape[-1] // 2
    inv_freq = rope_base ** (-2.0 * jnp.arange(half_dim, dtype=jnp.float32) / values.shape[-1])
    angles = positions.astype(jnp.float32)[:, None, None] * inv_freq
    cosine = jnp.cos(angles)
    sine = sign * jnp.sin(angles)
    first_half = values[..., :half_dim]
    second_half = values[..., half_dim:]
    return jnp.concatenate(
        [first_half * cosine - second_half * sine, second_half * cosine + first_half * sine],
        axis=-1,
    )


def visibility(segment_row, q_first, span_len):
    key_places = jnp.arange(segment_row.shape[0], dtype=jnp.int32)
    query_places = q_first + jnp.arange(span_len, dtype=jnp.int32)
    query_segs = lax.dynamic_slice_in_dim(segment_row, q_first, span_len)
    return (query_segs[:, None] == segment_row[None, :]) & (
        key_places[None, :] <= query_places[:, None]
    )


def masked_scores(grouped, keys, visible):
    scores = jnp.einsum(
        "qhgd,khd->hgqk", grouped, keys, preferred_element_type=jnp.float32
    ) * DH ** (-0.5)
    return jnp.where(visible, scores, -1e30)


def local(
    tokens,
    segments,
    positions,
    attn_gain,
    w_query,
    w_key,
    w_value,
    w_out,
    qk_gain,
    mlp_gain,
    w_gate,
    w_up,
    w_down,
    cotangent,
):
    seq_count, span_len, _ = tokens.shape
    row_count = seq_count * span_len
    heads_per = HQ // HK
    q_first = lax.axis_index("ctx") * span_len
    pos_flat = positions.reshape(row_count)
    g_attn, wq_full, wk_full, wv_full, wo_full = (
        lax.all_gather(attn_gain, ("dp", "ctx"), axis=0, tiled=True),
        lax.all_gather(w_query, ("dp", "ctx"), axis=0, tiled=True),
        lax.all_gather(w_key, ("dp", "ctx"), axis=0, tiled=True),
        lax.all_gather(w_value, ("dp", "ctx"), axis=0, tiled=True),
        lax.all_gather(w_out, ("dp", "ctx"), axis=0, tiled=True),
    )
    resid_in = tokens.reshape(row_count, D).astype(jnp.float32)
    normed_f, factor_in = norm_rows(resid_in, g_attn.astype(jnp.float32))
    normed = normed_f.astype(jnp.bfloat16)
    q_proj = jnp.dot(normed, wq_full, preferred_element_type=jnp.float32).reshape(row_count, HQ, DH)
    k_proj = jnp.dot(normed, wk_full, preferred_element_type=jnp.float32).reshape(row_count, HK, DH)
    v_low = (
        jnp.dot(normed, wv_full, preferred_element_type=jnp.float32)
        .astype(jnp.bfloat16)
        .reshape(seq_count, span_len, HK, DH)
    )
    gains_qk = qk_gain.astype(jnp.float32)
    q_norm, factor_q = norm_rows(q_proj, gains_qk[0])
    k_norm, factor_k = norm_rows(k_proj, gains_qk[1])
    q_low = rotate(q_norm, pos_flat, 1.0).astype(jnp.bfloat16).reshape(seq_count, span_len, HQ, DH)
    k_low = rotate(k_norm, pos_flat, 1.0).astype(jnp.bfloat16).reshape(seq_count, span_len, HK, DH)
    keys_all, values_all = (
        lax.all_gather(k_low, "ctx", axis=1, tiled=True),
        lax.all_gather(v_low, "ctx", axis=1, tiled=True),
    )

    def attend_forward(group_item):
        queries, keys, values, segment_row = group_item
        visible = visibility(segment_row, q_first, span_len)
        grouped = queries.reshape(span_len, HK, heads_per, DH)
        scores = masked_scores(grouped, keys, visible)
        row_max = jnp.max(scores, axis=-1, keepdims=True)
        weights = jnp.exp(scores - row_max)
        row_total = jnp.sum(weights, axis=-1, keepdims=True)
        prob_low = (weights / row_total).astype(jnp.bfloat16)
        attn_mix = jnp.einsum(
            "hgqk,khd->qhgd", prob_low, values, preferred_element_type=jnp.float32
        )
        return (
            attn_mix.reshape(span_len, HQ * DH).astype(jnp.bfloat16),
            row_max + jnp.log(row_total),
        )

    attn_mix, log_total = lax.map(attend_forward, (q_low, keys_all, values_all, segments))
    attn_mix = attn_mix.reshape(row_count, HQ * DH)
    hidden_in = resid_in + jnp.einsum(
        "th,dh->td", attn_mix, wo_full, preferred_element_type=jnp.float32
    )
    g_mlp, wg_full, wu_full, wd_full = (
        lax.all_gather(mlp_gain, ("dp", "ctx"), axis=0, tiled=True),
        lax.all_gather(w_gate, ("dp", "ctx"), axis=0, tiled=True),
        lax.all_gather(w_up, ("dp", "ctx"), axis=0, tiled=True),
        lax.all_gather(w_down, ("dp", "ctx"), axis=0, tiled=True),
    )
    normed_mlp_f, factor_mlp = norm_rows(hidden_in, g_mlp.astype(jnp.float32))
    normed_mlp = normed_mlp_f.astype(jnp.bfloat16)
    gated = jnp.dot(normed_mlp, wg_full, preferred_element_type=jnp.float32)
    upward = jnp.dot(normed_mlp, wu_full, preferred_element_type=jnp.float32)
    sigmoid_gate = jax.nn.sigmoid(gated)
    silu_gate = gated * sigmoid_gate
    inner = (silu_gate * upward).astype(jnp.bfloat16)
    result = hidden_in + jnp.einsum("tf,df->td", inner, wd_full, preferred_element_type=jnp.float32)
    layer_out = result.astype(jnp.bfloat16).reshape(seq_count, span_len, D)
    g_mlp, wg_full, wu_full, wd_full = (
        lax.all_gather(mlp_gain, ("dp", "ctx"), axis=0, tiled=True),
        lax.all_gather(w_gate, ("dp", "ctx"), axis=0, tiled=True),
        lax.all_gather(w_up, ("dp", "ctx"), axis=0, tiled=True),
        lax.all_gather(w_down, ("dp", "ctx"), axis=0, tiled=True),
    )
    grad_out = cotangent.reshape(row_count, D)
    grad_inner = jnp.dot(grad_out, wd_full, preferred_element_type=jnp.float32)
    grad_gate = (grad_inner * upward * sigmoid_gate * (1.0 + gated * (1.0 - sigmoid_gate))).astype(
        jnp.bfloat16
    )
    grad_up = (grad_inner * silu_gate).astype(jnp.bfloat16)
    grad_normed_mlp = jnp.einsum(
        "tf,df->td", grad_gate, wg_full, preferred_element_type=jnp.float32
    )
    grad_normed_mlp = grad_normed_mlp + jnp.einsum(
        "tf,df->td", grad_up, wu_full, preferred_element_type=jnp.float32
    )
    mlp_gain_part, grad_resid_mlp = norm_back(
        hidden_in, factor_mlp, g_mlp.astype(jnp.float32), grad_normed_mlp
    )
    d_w_down = jnp.einsum("td,tf->df", grad_out, inner, preferred_element_type=jnp.float32)
    d_w_gate = jnp.einsum("td,tf->df", normed_mlp, grad_gate, preferred_element_type=jnp.float32)
    d_w_up = jnp.einsum("td,tf->df", normed_mlp, grad_up, preferred_element_type=jnp.float32)
    d_mlp_gain, d_w_gate, d_w_up, d_w_down = (
        lax.psum_scatter(mlp_gain_part, ("dp", "ctx"), scatter_dimension=0, tiled=True),
        lax.psum_scatter(d_w_gate, ("dp", "ctx"), scatter_dimension=0, tiled=True),
        lax.psum_scatter(d_w_up, ("dp", "ctx"), scatter_dimension=0, tiled=True),
        lax.psum_scatter(d_w_down, ("dp", "ctx"), scatter_dimension=0, tiled=True),
    )
    grad_hidden = grad_out.astype(jnp.float32) + grad_resid_mlp
    g_attn, wq_full, wk_full, wv_full, wo_full = (
        lax.all_gather(attn_gain, ("dp", "ctx"), axis=0, tiled=True),
        lax.all_gather(w_query, ("dp", "ctx"), axis=0, tiled=True),
        lax.all_gather(w_key, ("dp", "ctx"), axis=0, tiled=True),
        lax.all_gather(w_value, ("dp", "ctx"), axis=0, tiled=True),
        lax.all_gather(w_out, ("dp", "ctx"), axis=0, tiled=True),
    )
    grad_attn = grad_hidden.astype(jnp.bfloat16)
    grad_mix = jnp.einsum(
        "td,dh->th", grad_attn, wo_full, preferred_element_type=jnp.float32
    ).astype(jnp.bfloat16)
    grad_mix = grad_mix.reshape(seq_count, span_len, HQ, DH)

    def attend_backward(group_item):
        queries, keys, values, grad_rows, log_rows, segment_row = group_item
        visible = visibility(segment_row, q_first, span_len)
        grouped = queries.reshape(span_len, HK, heads_per, DH)
        scores = masked_scores(grouped, keys, visible)
        probs = jnp.exp(scores - log_rows)
        grad_group = grad_rows.reshape(span_len, HK, heads_per, DH)
        grad_probs = jnp.einsum(
            "qhgd,khd->hgqk", grad_group, values, preferred_element_type=jnp.float32
        )
        center = jnp.sum(probs * grad_probs, axis=-1, keepdims=True)
        grad_scores = (probs * (grad_probs - center)).astype(jnp.bfloat16)
        grad_q = jnp.einsum(
            "hgqk,khd->qhgd", grad_scores, keys, preferred_element_type=jnp.float32
        ) * DH ** (-0.5)
        grad_k = jnp.einsum(
            "hgqk,qhgd->khd", grad_scores, grouped, preferred_element_type=jnp.float32
        ) * DH ** (-0.5)
        grad_v = jnp.einsum(
            "hgqk,qhgd->khd",
            probs.astype(jnp.bfloat16),
            grad_group,
            preferred_element_type=jnp.float32,
        )
        return (grad_q.reshape(span_len, HQ, DH), grad_k, grad_v)

    grad_q, grad_k_all, grad_v_all = lax.map(
        attend_backward, (q_low, keys_all, values_all, grad_mix, log_total, segments)
    )
    grad_k, grad_v = (
        lax.psum_scatter(
            grad_k_all.astype(jnp.bfloat16), "ctx", scatter_dimension=1, tiled=True
        ).astype(jnp.float32),
        lax.psum_scatter(
            grad_v_all.astype(jnp.bfloat16), "ctx", scatter_dimension=1, tiled=True
        ).astype(jnp.float32),
    )
    grad_qn = rotate(grad_q.reshape(row_count, HQ, DH), pos_flat, -1.0)
    grad_kn = rotate(grad_k.reshape(row_count, HK, DH), pos_flat, -1.0)
    q_gain_part, grad_qp = norm_back(q_proj, factor_q, gains_qk[0], grad_qn)
    k_gain_part, grad_kp = norm_back(k_proj, factor_k, gains_qk[1], grad_kn)
    grad_q_low = grad_qp.reshape(row_count, HQ * DH).astype(jnp.bfloat16)
    grad_k_low = grad_kp.reshape(row_count, HK * DH).astype(jnp.bfloat16)
    grad_v_low = grad_v.reshape(row_count, HK * DH).astype(jnp.bfloat16)
    grad_normed = jnp.einsum("th,dh->td", grad_q_low, wq_full, preferred_element_type=jnp.float32)
    grad_normed = grad_normed + jnp.einsum(
        "th,dh->td", grad_k_low, wk_full, preferred_element_type=jnp.float32
    )
    grad_normed = grad_normed + jnp.einsum(
        "th,dh->td", grad_v_low, wv_full, preferred_element_type=jnp.float32
    )
    attn_gain_part, grad_resid_attn = norm_back(
        resid_in, factor_in, g_attn.astype(jnp.float32), grad_normed
    )
    d_qk_gain = lax.psum(jnp.stack([q_gain_part, k_gain_part]), ("dp", "ctx"))
    d_w_out = jnp.einsum("td,th->dh", grad_attn, attn_mix, preferred_element_type=jnp.float32)
    d_w_query = jnp.einsum("td,th->dh", normed, grad_q_low, preferred_element_type=jnp.float32)
    d_w_key = jnp.einsum("td,th->dh", normed, grad_k_low, preferred_element_type=jnp.float32)
    d_w_value = jnp.einsum("td,th->dh", normed, grad_v_low, preferred_element_type=jnp.float32)
    d_attn_gain, d_w_query, d_w_key, d_w_value, d_w_out = (
        lax.psum_scatter(attn_gain_part, ("dp", "ctx"), scatter_dimension=0, tiled=True),
        lax.psum_scatter(d_w_query, ("dp", "ctx"), scatter_dimension=0, tiled=True),
        lax.psum_scatter(d_w_key, ("dp", "ctx"), scatter_dimension=0, tiled=True),
        lax.psum_scatter(d_w_value, ("dp", "ctx"), scatter_dimension=0, tiled=True),
        lax.psum_scatter(d_w_out, ("dp", "ctx"), scatter_dimension=0, tiled=True),
    )
    d_tokens = (grad_hidden + grad_resid_attn).reshape(seq_count, span_len, D)
    return (
        layer_out,
        d_tokens,
        d_attn_gain,
        d_w_query,
        d_w_key,
        d_w_value,
        d_w_out,
        d_qk_gain,
        d_mlp_gain,
        d_w_gate,
        d_w_up,
        d_w_down,
    )


AXES = ("dp", "ctx")
SCALE = DH ** (-0.5)
LOG2E = math.log2(math.e)
NEG = -1e30
BF = jnp.bfloat16
F32 = jnp.float32


class Place:
    def __init__(self, dp_size, ctx_size):
        self.count = dp_size * ctx_size
        self.z_size = ctx_size
        dp = lax.axis_index("dp")
        self.z = lax.axis_index("ctx")
        self.c = dp % 2
        self.x = (dp // 2) % 2
        self.y = dp // 4

    def split(self, flat):
        z, dp = flat % self.z_size, flat // self.z_size
        return dp // 4, (dp // 2) % 2, dp % 2, z

    def join(self, y, x, c, z):
        return ((y * 2 + x) * 2 + c) * self.z_size + z

    def move(self, values, target):
        perm = []
        for flat in range(self.count):
            perm.append((flat, self.join(*target(*self.split(flat)))))
        return lax.ppermute(values, AXES, perm)

    def swap(self, values, axis):
        return self.move(
            values,
            lambda y, x, c, z: (
                1 - y if axis == "y" else y,
                1 - x if axis == "x" else x,
                1 - c if axis == "c" else c,
                z,
            ),
        )

    def shift(self, values, step):
        return self.move(values, lambda y, x, c, z: (y, x, c, (z + step) % self.z_size))


def arrived(earlier):
    first = earlier[(0,) * earlier.ndim]
    return (first != first).astype(jnp.int32)


def all_arrived(*earlier):
    return sum(arrived(one) for one in earlier).reshape(1)


def hold(late, values):
    return jnp.where(late == 0, values, jnp.zeros_like(values))


STRETCHES = ((0, 3), (1, 2))
CORE_OF = (0, 1, 1, 0)
RANK_OF = (0, 0, 1, 1)


def rank_here(place):
    return jnp.asarray(RANK_OF, jnp.int32)[place.z]


def to_sequences(place, values, late=0):
    parts = []
    for m in range(2):
        chosen = pick(values, (rank_here(place) + m) % 2 + 2 * late, 0)
        parts.append(
            place.move(
                chosen, lambda y, x, c, z: (y, x, CORE_OF[z], 2 * c + (RANK_OF[z] + m) % 2)
            )
        )
    first, second = parts
    even = place.z % 2 == 0
    return jnp.concatenate(
        [jnp.where(even, first, second), jnp.where(even, second, first)], axis=0
    )


def from_sequences(place, values, late=0):
    parts = []
    for m in range(2):
        chosen = pick(values, (m + place.z) % 2 + 2 * late, 0)
        parts.append(
            place.move(
                chosen,
                lambda y, x, c, z: (y, x, z // 2, STRETCHES[c][(m + z) % 2]),
            )
        )
    first, second = parts
    even = rank_here(place) == 0
    return jnp.stack([jnp.where(even, first, second), jnp.where(even, second, first)])


def gather_z(place, shards, late=0):
    widths = [shard.shape[1] for shard in shards]
    shard = jnp.concatenate(shards, axis=1)
    shard = jnp.where(late == 0, shard, jnp.zeros_like(shard))
    pieces = [shard]
    for _ in range(1, place.z_size):
        pieces.append(place.shift(pieces[-1], 1))
    start, stacks = 0, []
    for width in widths:
        stacks.append(jnp.stack([piece[:, start : start + width] for piece in pieces]))
        start += width
    return stacks, pieces


class Lanes:
    def __init__(self):
        self.last = {}

    def late(self, axis):
        return arrived(self.last[axis]) if axis in self.last else jnp.int32(0)

    def swap(self, place, values, axis):
        self.last[axis] = place.swap(values, axis)
        return self.last[axis]


def gather_pair(place, lanes, one, two, *earlier):
    if earlier:
        one = jnp.where(arrived(earlier[0]) == 0, one, jnp.zeros_like(one))
        two = jnp.where(arrived(earlier[1]) == 0, two, jnp.zeros_like(two))
    one = jnp.stack([one, lanes.swap(place, one, "x")])
    two = jnp.stack([two, lanes.swap(place, two, "y")])
    one_far = lanes.swap(place, one, "y")
    two_far = lanes.swap(place, two, "x")
    return tuple(
        (near, far, place.swap(near, "c"), place.swap(far, "c"))
        for near, far in ((one, one_far), (two, two_far))
    )


def assemble(place, quarters, second_axis, widths):
    z_size, rows, total = place.z_size, quarters[0].shape[2], quarters[0].shape[3]
    first_is_x = second_axis == "y"
    here = jnp.stack(
        [place.x if first_is_x else place.y, place.y if first_is_x else place.x, place.c, place.z]
    ).astype(jnp.int32)

    def kernel(here_ref, near, far, near_core, far_core, *outs):
        second, core = here_ref[1], here_ref[2]
        for ref, from_second, from_core in (
            (near, 0, 0),
            (far, 1, 0),
            (near_core, 0, 1),
            (far_core, 1, 1),
        ):
            at_second = lax.rem(second + from_second, 2)
            at_core = lax.rem(core + from_core, 2)
            start = 0
            for out, width in zip(outs, widths):
                block = ref[0, 0, :, start : start + width]
                if first_is_x:
                    out[at_second, 0, at_core, 0] = block
                else:
                    out[0, at_second, at_core, 0] = block
                start += width

    def in_map(i, k, here_ref):
        return (i, k, 0, 0)

    def out_map(i, k, here_ref):
        first = lax.rem(here_ref[0] + i, 2)
        z = lax.rem(here_ref[3] + z_size - k, z_size)
        return (0, first, 0, z, 0, 0) if first_is_x else (first, 0, 0, z, 0, 0)

    def out_block(width):
        return (2, 1, 2, 1, rows, width) if first_is_x else (1, 2, 2, 1, rows, width)

    outs = pl.pallas_call(
        kernel,
        grid_spec=pltpu.PrefetchScalarGridSpec(
            num_scalar_prefetch=1,
            grid=(2, z_size),
            in_specs=[pl.BlockSpec((1, 1, rows, total), in_map)] * 4,
            out_specs=[pl.BlockSpec(out_block(width), out_map) for width in widths],
        ),
        out_shape=[
            jax.ShapeDtypeStruct((2, 2, 2, z_size, rows, width), BF) for width in widths
        ],
        compiler_params=pltpu.CompilerParams(vmem_limit_bytes=32 * 2**20),
        cost_estimate=pl.CostEstimate(
            flops=0, bytes_accessed=2 * 8 * z_size * rows * total * 2, transcendentals=0
        ),
        name="assemble",
    )(here, *quarters)
    return [out.reshape(8 * z_size * rows, out.shape[-1]) for out in outs]


def pick(values, index, axis):
    return lax.dynamic_index_in_dim(values, index, axis, keepdims=False)


def arrange(place, values, late=None):
    rows, width = values.shape
    z_size, part = place.z_size, width // place.count
    here = jnp.stack([place.c, place.x, place.y, place.z]).astype(jnp.int32)
    if late is not None:
        here = here + late

    width_z = z_size * part

    def kernel(here_ref, in_ref, out_x_ref, out_y_ref):
        for core in range(2):
            for at_x in range(2):
                for at_y in range(2):
                    c, x, y = (
                        lax.rem(here_ref[k] + at, 2) for k, at in enumerate((core, at_x, at_y))
                    )
                    start = pl.multiple_of(((y * 2 + x) * 2 + c) * width_z, width_z)
                    turned = pltpu.roll(
                        in_ref[:, pl.ds(start, width_z)].astype(F32),
                        lax.rem(z_size - here_ref[3], z_size) * part,
                        1,
                    ).astype(BF)
                    for out_ref, place_of in (
                        (out_x_ref, core * 4 + at_x * 2 + at_y),
                        (out_y_ref, core * 4 + at_y * 2 + at_x),
                    ):
                        out_ref[:, place_of * width_z : (place_of + 1) * width_z] = turned

    whole = pl.BlockSpec((rows, width), lambda i, here_ref: (0, 0))
    out_x, out_y = pl.pallas_call(
        kernel,
        grid_spec=pltpu.PrefetchScalarGridSpec(
            num_scalar_prefetch=1, grid=(1,), in_specs=[whole], out_specs=[whole, whole]
        ),
        out_shape=[jax.ShapeDtypeStruct((rows, width), BF)] * 2,
        compiler_params=pltpu.CompilerParams(vmem_limit_bytes=32 * 2**20),
        cost_estimate=pl.CostEstimate(
            flops=0, bytes_accessed=6 * rows * width, transcendentals=0
        ),
        name="arrange",
    )(here, values)
    return {"xy": out_x, "yx": out_y}


TN = (((0,), (0,)), ((), ()))


class Reduction:
    def __init__(self, place, left, right, axes):
        self.place, self.left, self.right, self.axes = place, left[axes], right, axes
        self.half = self.left.shape[1] // 2

    def product(self, start, end):
        return dot32(self.left[:, start:end], self.right, TN)

    def core(self):
        half = self.half
        sent = self.product(half, 2 * half).astype(BF)
        self.from_core = self.place.swap(sent, "c")
        return self.from_core

    def first(self):
        half = self.half
        sent = self.product(half // 2, half) + self.from_core[half // 2 :].astype(F32)
        self.from_first = self.place.swap(sent.astype(BF), self.axes[0])
        return self.from_first

    def second(self):
        quarter = self.half // 2
        total = self.product(0, quarter) + self.from_core[:quarter].astype(F32)
        total = (total + self.from_first.astype(F32)).astype(BF)
        self.kept = total[: quarter // 2]
        self.from_second = self.place.swap(total[quarter // 2 :], self.axes[1])
        return self.from_second

    def rest(self):
        return (self.kept.astype(F32) + self.from_second.astype(F32)).astype(BF)


def finish_rows(place, parts):
    rows = parts.shape[0] // place.z_size
    total = parts[:rows].astype(F32)
    for k in range(1, place.z_size):
        total = total + place.shift(parts[k * rows : (k + 1) * rows], k).astype(F32)
    return total


def sum_everywhere(place, values):
    for axis in ("c", "y", "x"):
        values = values + place.swap(values, axis)
    step = 1
    while step < place.z_size:
        values = values + place.move(values, lambda y, x, c, z: (y, x, c, z ^ step))
        step *= 2
    return values


def head_factor(values):
    return lax.rsqrt(jnp.mean(values * values, axis=-1, keepdims=True) + norm_eps)


def head_back(values, gain, upstream):
    factor = head_factor(values)
    weighted = upstream * gain
    gain_grad = jnp.sum(upstream * values * factor, axis=0, keepdims=True)
    inner_mean = jnp.mean(weighted * values, axis=-1, keepdims=True)
    return gain_grad, factor * weighted - values * factor * factor * factor * inner_mean


def turn(values, cosine, sine):
    return values * cosine + pltpu.roll(values, DH // 2, 1) * sine


def prepare_kv(kv_proj, gain, cosine, sine):
    rows = kv_proj.shape[0]

    def kernel(k_ref, v_ref, gain_ref, cos_ref, sin_ref, out_ref):
        values = k_ref[...]
        normed = values * head_factor(values) * gain_ref[...]
        out_ref[0] = turn(normed, cos_ref[...], sin_ref[...]).astype(BF)
        out_ref[1] = v_ref[...].astype(BF)

    whole = lambda shape: pl.BlockSpec(shape, lambda h: (0, 0))
    return pl.pallas_call(
        kernel,
        grid=(HK,),
        in_specs=[
            pl.BlockSpec((rows, DH), lambda h: (0, h)),
            pl.BlockSpec((rows, DH), lambda h: (0, HK + h)),
            whole((1, DH)),
            whole((rows, DH)),
            whole((rows, DH)),
        ],
        out_specs=pl.BlockSpec((2, rows, DH), lambda h: (0, 0, h)),
        out_shape=jax.ShapeDtypeStruct((2, rows, HK * DH), BF),
        cost_estimate=pl.CostEstimate(
            flops=10 * rows * HK * DH, bytes_accessed=12 * rows * HK * DH, transcendentals=0
        ),
        name="prepare_kv",
    )(kv_proj, kv_proj, gain, cosine, sine)


def finish_kv(late, kv_proj, own, received, gain, cosine, sine):
    rows = kv_proj.shape[0]

    def kernel(late_ref, k_ref, own_ref, other_ref, gain_ref, cos_ref, sin_ref, out_ref, gain_out):
        @pl.when(pl.program_id(0) == 0)
        def _():
            gain_out[...] = jnp.zeros_like(gain_out)

        grad_k = own_ref[0] + other_ref[0].astype(F32)
        grad_kn = turn(grad_k, cos_ref[...], -sin_ref[...])
        gain_grad, grad_kp = head_back(k_ref[...], gain_ref[...], grad_kn)
        gain_out[...] += gain_grad
        out_ref[0] = grad_kp.astype(BF)
        out_ref[1] = (own_ref[1] + other_ref[1].astype(F32)).astype(BF)

    whole = lambda shape: pl.BlockSpec(shape, lambda h: (0, 0))
    pair = pl.BlockSpec((2, rows, DH), lambda h: (0, 0, h))
    return pl.pallas_call(
        kernel,
        grid=(HK,),
        in_specs=[
            pl.BlockSpec(memory_space=pltpu.SMEM),
            pl.BlockSpec((rows, DH), lambda h: (0, h)),
            pair,
            pair,
            whole((1, DH)),
            whole((rows, DH)),
            whole((rows, DH)),
        ],
        out_specs=[pair, whole((1, DH))],
        out_shape=[
            jax.ShapeDtypeStruct((2, rows, HK * DH), BF),
            jax.ShapeDtypeStruct((1, DH), F32),
        ],
        cost_estimate=pl.CostEstimate(
            flops=30 * rows * HK * DH, bytes_accessed=20 * rows * HK * DH, transcendentals=0
        ),
        name="finish_kv",
    )(late, kv_proj, own, received, gain, cosine, sine)


def interleave(own, other):
    half = own.shape[0] // 2
    return jnp.concatenate([own[:half], other[:half], own[half:], other[half:]], axis=0)


def fill_bias(q_ref, k_ref, bias_ref):
    bias_ref[...] = jnp.where(
        (k_ref[:, 0:1] <= q_ref[0:1, :]) & (k_ref[:, 1:2] == q_ref[1:2, :]), 0.0, NEG
    ).astype(F32)


NT = (((1,), (1,)), ((), ()))
NN = (((1,), (0,)), ((), ()))


def dot32(left, right, dims):
    return lax.dot_general(left, right, dims, preferred_element_type=F32)


def attend_fwd(q_proj, own_kv, other_kv, gain, cosine, sine, q_codes, k_codes):
    rows = q_proj.shape[0]
    half = rows // 2
    keys_n = 2 * rows

    def kernel(
        q_ref, own_ref, other_ref, gain_ref, cos_ref, sin_ref, qc_ref, kc_ref,
        mix_ref, q_low_ref, total_ref, bias_ref,
    ):
        @pl.when(pl.program_id(0) == 0)
        def _():
            fill_bias(qc_ref, kc_ref, bias_ref)

        heads = []
        for g in range(2):
            values = q_ref[:, g * DH : (g + 1) * DH]
            normed = values * head_factor(values) * gain_ref[...]
            low = turn(normed, cos_ref[...], sin_ref[...]).astype(BF)
            q_low_ref[:, g * DH : (g + 1) * DH] = low
            heads.append(low)
        keys = interleave(own_ref[0], other_ref[0])
        values_t = interleave(own_ref[1], other_ref[1]).T
        for part in range(2):
            span = slice(part * half, (part + 1) * half)
            count = keys_n if part else rows
            queries = jnp.concatenate([heads[0][span], heads[1][span]], axis=0)
            bias = bias_ref[:count, span]
            scores = dot32(keys[:count], queries, NT) * (SCALE * LOG2E) + jnp.concatenate(
                [bias, bias], axis=1
            )
            row_max = jnp.max(scores, axis=0, keepdims=True)
            weights = jnp.exp2(scores - row_max)
            row_total = jnp.sum(weights, axis=0, keepdims=True)
            mix_t = dot32(values_t[:, :count], weights.astype(BF), NN) / row_total
            mix = mix_t.T.astype(BF)
            mix_ref[span, :DH] = mix[:half]
            mix_ref[span, DH:] = mix[half:]
            total_ref[0, part : part + 1, :] = row_max + jnp.log2(row_total)

    whole = lambda shape: pl.BlockSpec(shape, lambda h: (0, 0))
    pair = pl.BlockSpec((2, rows, DH), lambda h: (0, 0, h))
    wide = pl.BlockSpec((rows, 2 * DH), lambda h: (0, h))
    return pl.pallas_call(
        kernel,
        grid=(HK,),
        in_specs=[
            wide, pair, pair, whole((1, DH)), whole((rows, DH)), whole((rows, DH)),
            whole((2, rows)), whole((keys_n, 2)),
        ],
        out_specs=[wide, wide, pl.BlockSpec((1, 2, rows), lambda h: (h, 0, 0))],
        out_shape=[
            jax.ShapeDtypeStruct((rows, HQ * DH), BF),
            jax.ShapeDtypeStruct((rows, HQ * DH), BF),
            jax.ShapeDtypeStruct((HK, 2, rows), F32),
        ],
        scratch_shapes=[pltpu.VMEM((keys_n, rows), F32)],
        compiler_params=pltpu.CompilerParams(vmem_limit_bytes=48 * 2**20),
        cost_estimate=pl.CostEstimate(
            flops=HK * 2 * 2 * rows * 3 * rows * DH,
            bytes_accessed=16 * 2**20,
            transcendentals=HK * rows * 3 * rows,
        ),
        name="attend_fwd",
    )(q_proj, own_kv, other_kv, gain, cosine, sine, q_codes, k_codes)


def attend_bwd(
    late, q_proj, q_low, own_kv, other_kv, grad_mix, totals, gain, cosine, sine, q_codes, k_codes
):
    rows = q_proj.shape[0]
    half = rows // 2
    keys_n = 2 * rows

    def kernel(
        late_ref, q_ref, q_low_ref, own_ref, other_ref, grad_ref, total_ref, gain_ref, cos_ref, sin_ref,
        qc_ref, kc_ref, grad_q_ref, grad_own_ref, grad_other_ref, gain_out, bias_ref,
    ):
        @pl.when(pl.program_id(0) == 0)
        def _():
            fill_bias(qc_ref, kc_ref, bias_ref)
            gain_out[...] = jnp.zeros_like(gain_out)

        keys = interleave(own_ref[0], other_ref[0])
        keys_t = keys.T
        values = interleave(own_ref[1], other_ref[1])
        parts_q, parts_k, parts_v = [], [], []
        for part in range(2):
            span = slice(part * half, (part + 1) * half)
            count = keys_n if part else rows
            queries = jnp.concatenate([q_low_ref[span, :DH], q_low_ref[span, DH:]], axis=0)
            grads = jnp.concatenate([grad_ref[span, :DH], grad_ref[span, DH:]], axis=0)
            bias = bias_ref[:count, span]
            scores = dot32(keys[:count], queries, NT) * (SCALE * LOG2E) + jnp.concatenate(
                [bias, bias], axis=1
            )
            probs = jnp.exp2(scores - total_ref[0, part : part + 1, :])
            grad_probs = dot32(values[:count], grads, NT)
            product = probs * grad_probs
            center = jnp.sum(product, axis=0, keepdims=True)
            grad_scores = (product - probs * center).astype(BF)
            parts_v.append(dot32(probs.astype(BF), grads, NN))
            parts_k.append(dot32(grad_scores, queries, NN) * SCALE)
            parts_q.append(dot32(keys_t[:, :count], grad_scores, NN).T * SCALE)
        for slot, parts in ((0, parts_k), (1, parts_v)):
            low_part, high_part = parts
            both = high_part[:rows] + low_part
            grad_own_ref[slot, :half] = both[:half]
            grad_other_ref[slot, :half] = both[half:].astype(BF)
            grad_own_ref[slot, half:] = high_part[rows : rows + half]
            grad_other_ref[slot, half:] = high_part[rows + half :].astype(BF)
        gain_total = gain_out[...]
        for g in range(2):
            grad_q = jnp.concatenate(
                [parts_q[0][g * half : (g + 1) * half], parts_q[1][g * half : (g + 1) * half]],
                axis=0,
            )
            grad_qn = turn(grad_q, cos_ref[...], -sin_ref[...])
            gain_grad, grad_qp = head_back(
                q_ref[:, g * DH : (g + 1) * DH], gain_ref[...], grad_qn
            )
            gain_total += gain_grad
            grad_q_ref[:, g * DH : (g + 1) * DH] = grad_qp.astype(BF)
        gain_out[...] = gain_total

    whole = lambda shape: pl.BlockSpec(shape, lambda h: (0, 0))
    pair = pl.BlockSpec((2, rows, DH), lambda h: (0, 0, h))
    wide = pl.BlockSpec((rows, 2 * DH), lambda h: (0, h))
    return pl.pallas_call(
        kernel,
        grid=(HK,),
        in_specs=[
            pl.BlockSpec(memory_space=pltpu.SMEM),
            wide, wide, pair, pair, wide, pl.BlockSpec((1, 2, rows), lambda h: (h, 0, 0)),
            whole((1, DH)), whole((rows, DH)), whole((rows, DH)),
            whole((2, rows)), whole((keys_n, 2)),
        ],
        out_specs=[wide, pair, pair, whole((1, DH))],
        out_shape=[
            jax.ShapeDtypeStruct((rows, HQ * DH), BF),
            jax.ShapeDtypeStruct((2, rows, HK * DH), F32),
            jax.ShapeDtypeStruct((2, rows, HK * DH), BF),
            jax.ShapeDtypeStruct((1, DH), F32),
        ],
        scratch_shapes=[pltpu.VMEM((keys_n, rows), F32)],
        compiler_params=pltpu.CompilerParams(vmem_limit_bytes=56 * 2**20),
        cost_estimate=pl.CostEstimate(
            flops=HK * 5 * 2 * rows * 3 * rows * DH,
            bytes_accessed=24 * 2**20,
            transcendentals=HK * rows * 3 * rows,
        ),
        name="attend_bwd",
    )(late, q_proj, q_low, own_kv, other_kv, grad_mix, totals, gain, cosine, sine, q_codes, k_codes)


def mm(left, right, dims):
    return jnp.einsum(dims, left, right, preferred_element_type=F32)


def chip_local(
    dp_size, ctx_size,
    tokens, segments, positions, attn_gain, w_query, w_key, w_value, w_out, qk_gain, mlp_gain,
    w_gate, w_up, w_down, cotangent,
):
    place = Place(dp_size, ctx_size)
    _, stretch, _ = tokens.shape
    rows = 2 * stretch
    spread = lambda gain: jnp.broadcast_to(gain[:, None], (gain.shape[0], 128))

    lanes = Lanes()
    spread_kv = jnp.concatenate([w_key, w_value, spread(attn_gain)], axis=1)
    spread_up = jnp.concatenate([w_up, spread(mlp_gain)], axis=1)
    (z_q, z_kv), came = gather_z(place, [w_query, spread_kv])
    seq_tokens = to_sequences(place, tokens, arrived(came[-1]))
    other_segments = place.swap(segments, "c")
    four_q, four_kv = gather_pair(place, lanes, z_q, z_kv)
    seq_positions = to_sequences(place, positions, arrived(four_kv[1]))
    (z_out, z_up), came = gather_z(
        place, [w_out, spread_up], arrived(seq_tokens) + arrived(four_q[0]) + arrived(four_kv[0])
    )
    four_out, four_up = gather_pair(place, lanes, z_out, z_up, four_kv[3], four_q[3])
    (z_gate, z_down), came = gather_z(
        place, [w_gate, w_down], arrived(four_out[0]) + arrived(four_up[0])
    )
    four_gate, four_down = gather_pair(
        place, lanes, z_gate, z_down, lanes.last["x"], lanes.last["y"]
    )
    seq_cotangent = to_sequences(place, cotangent, arrived(four_gate[0]) + arrived(four_down[0]))
    kv_full, g_attn = assemble(place, four_kv, "x", (2 * HK * DH, 128))
    (q_full,) = assemble(place, four_q, "y", (HQ * DH,))
    (out_full,) = assemble(place, four_out, "y", (HQ * DH,))
    up_full, g_mlp = assemble(place, four_up, "x", (w_up.shape[1], 128))
    (gate_full,) = assemble(place, four_gate, "y", (w_gate.shape[1],))
    (down_full,) = assemble(place, four_down, "x", (w_down.shape[1],))
    g_attn = g_attn[:, 0].astype(F32)
    g_mlp = g_mlp[:, 0].astype(F32)

    segment_rows = jnp.where(place.z // 2 == place.c, segments, other_segments)
    segment_row = pick(segment_rows, place.z % 2, 0)
    within = jnp.arange(stretch, dtype=jnp.int32)
    near, far, other_near, other_far = (
        jnp.where(place.c == 0, left, right) for left, right in ((0, 1), (3, 2), (1, 0), (2, 3))
    )
    codes = [
        jnp.stack(
            [k * stretch + within, lax.dynamic_slice_in_dim(segment_row, k * stretch, stretch)]
        )
        for k in (near, other_near, far, other_far)
    ]
    q_codes = jnp.concatenate([codes[0], codes[2]], axis=1)
    k_codes = jnp.concatenate(codes, axis=1).T
    inv_freq = rope_base ** (-2.0 * jnp.arange(DH // 2, dtype=F32) / DH)
    angles = seq_positions.reshape(rows).astype(F32)[:, None] * inv_freq
    cosine, sine = jnp.cos(angles), jnp.sin(angles)
    cosine = jnp.concatenate([cosine, cosine], axis=1)
    sine = jnp.concatenate([-sine, sine], axis=1)
    gains_qk = qk_gain.astype(F32)
    q_gain, k_gain = gains_qk[0:1], gains_qk[1:2]

    resid_in = seq_tokens.reshape(rows, D).astype(F32)
    normed_f, factor_in = norm_rows(resid_in, g_attn)
    normed = normed_f.astype(BF)
    kv_proj = mm(normed, kv_full, "td,dh->th")
    own_kv = prepare_kv(kv_proj, k_gain, cosine, sine)
    other_kv = place.swap(own_kv, "c")
    q_proj = mm(normed, q_full, "td,dh->th")
    attn_mix, q_low, totals = attend_fwd(
        q_proj, own_kv, other_kv, q_gain, cosine, sine, q_codes, k_codes
    )
    hidden_in = resid_in + mm(attn_mix, out_full, "th,dh->td")
    normed_mlp_f, factor_mlp = norm_rows(hidden_in, g_mlp)
    normed_mlp = normed_mlp_f.astype(BF)
    gated = mm(normed_mlp, gate_full, "td,df->tf")
    upward = mm(normed_mlp, up_full, "td,df->tf")
    sigmoid_gate = jax.nn.sigmoid(gated)
    silu_gate = gated * sigmoid_gate
    inner = (silu_gate * upward).astype(BF)
    result = (hidden_in + mm(inner, down_full, "tf,df->td")).astype(BF)
    layer_out = from_sequences(place, result.reshape(2, stretch, D))

    grad_out = seq_cotangent.reshape(rows, D)
    middle = inner.shape[1] // 2
    by_out = arrange(place, grad_out)
    down_left = Reduction(place, by_out, inner[:, :middle], "xy")
    down_right = Reduction(place, by_out, inner[:, middle:], "yx")
    down_late = arrived(down_left.core()) + arrived(down_right.core())
    grad_inner = mm(grad_out, down_full, "td,df->tf")
    grad_gate = (grad_inner * upward * sigmoid_gate * (1.0 + gated * (1.0 - sigmoid_gate))).astype(BF)
    grad_up = (grad_inner * silu_gate).astype(BF)
    by_mlp = arrange(place, normed_mlp)
    gate = Reduction(place, by_mlp, grad_gate, "yx")
    up = Reduction(place, by_mlp, grad_up, "xy")
    waits = [gate.core(), up.core(), down_left.first(), down_right.first()]
    grad_normed_mlp = mm(grad_gate, gate_full, "tf,df->td") + mm(grad_up, up_full, "tf,df->td")
    grad_normed_mlp = hold(down_late, grad_normed_mlp)
    mlp_gain_part, grad_resid_mlp = norm_back(hidden_in, factor_mlp, g_mlp, grad_normed_mlp)
    grad_hidden = grad_out.astype(F32) + grad_resid_mlp

    grad_attn = grad_hidden.astype(BF)
    grad_mix = mm(grad_attn, out_full, "td,dh->th").astype(BF)
    grad_q_low, own_grad, other_grad, q_gain_part = attend_bwd(
        all_arrived(*waits),
        q_proj, q_low, own_kv, other_kv, grad_mix, totals, q_gain, cosine, sine, q_codes, k_codes,
    )
    received = place.swap(other_grad, "c")
    middle = attn_mix.shape[1] // 2
    by_attn = arrange(place, grad_attn)
    out_left = Reduction(place, by_attn, attn_mix[:, :middle], "xy")
    out_right = Reduction(place, by_attn, attn_mix[:, middle:], "yx")
    waits = [gate.first(), up.first(), out_left.core(), out_right.core()]
    grad_kv_low, k_gain_part = finish_kv(
        all_arrived(*waits), kv_proj, own_grad, received, k_gain, cosine, sine
    )
    grad_kv_low = jnp.concatenate([grad_kv_low[0], grad_kv_low[1]], axis=1)
    by_in = arrange(place, normed)
    query = Reduction(place, by_in, grad_q_low, "yx")
    kv = Reduction(place, by_in, grad_kv_low, "xy")
    starts = [query.core(), kv.core()]
    early = [gate, up, down_left, down_right]
    late = [query, kv, out_left, out_right]
    for one in early:
        one.second()
    for one in (query, kv, out_left, out_right):
        one.first()
    for one in (query, kv, out_left, out_right):
        one.second()
    d_early = finish_rows(place, jnp.concatenate([one.rest() for one in early], axis=1))
    d_late = finish_rows(place, jnp.concatenate([one.rest() for one in late], axis=1))
    ff, wide = w_gate.shape[1], HQ * DH
    d_gate, d_up, d_down = d_early[:, :ff], d_early[:, ff : 2 * ff], d_early[:, 2 * ff :]
    d_query, d_kv, d_out = d_late[:, :wide], d_late[:, wide : 2 * wide], d_late[:, 2 * wide :]
    grad_normed = mm(grad_q_low, q_full, "th,dh->td") + mm(grad_kv_low, kv_full, "th,dh->td")
    attn_gain_part, grad_resid_attn = norm_back(resid_in, factor_in, g_attn, grad_normed)
    d_seq = (grad_hidden + grad_resid_attn).astype(BF)
    d_tokens = from_sequences(place, d_seq.reshape(2, stretch, D)).astype(F32)

    small = jnp.concatenate(
        [attn_gain_part, mlp_gain_part, q_gain_part.reshape(DH), k_gain_part.reshape(DH)]
    )
    small = jnp.where(all_arrived(*starts)[0] == 0, small, 0.0)
    small = sum_everywhere(place, small.reshape(-1, 128)).reshape(-1)
    flat = lax.axis_index("dp") * ctx_size + lax.axis_index("ctx")
    own = D // place.count
    d_attn_gain = lax.dynamic_slice_in_dim(small, flat * own, own)
    d_mlp_gain = lax.dynamic_slice_in_dim(small, D + flat * own, own)
    d_qk_gain = small[2 * D :].reshape(2, DH)
    return (
        layer_out, d_tokens, d_attn_gain, d_query, d_kv[:, : HK * DH], d_kv[:, HK * DH :], d_out,
        d_qk_gain, d_mlp_gain, d_gate, d_up, d_down,
    )


def solution(mesh):
    in_specs = (
        P("dp", "ctx", None),
        P("dp", None),
        P("dp", "ctx"),
        P(("dp", "ctx")),
        P(("dp", "ctx"), None),
        P(("dp", "ctx"), None),
        P(("dp", "ctx"), None),
        P(("dp", "ctx"), None),
        P(),
        P(("dp", "ctx")),
        P(("dp", "ctx"), None),
        P(("dp", "ctx"), None),
        P(("dp", "ctx"), None),
        P("dp", "ctx", None),
    )
    out_specs = (
        P("dp", "ctx", None),
        P("dp", "ctx", None),
        P(("dp", "ctx")),
        P(("dp", "ctx"), None),
        P(("dp", "ctx"), None),
        P(("dp", "ctx"), None),
        P(("dp", "ctx"), None),
        P(),
        P(("dp", "ctx")),
        P(("dp", "ctx"), None),
        P(("dp", "ctx"), None),
        P(("dp", "ctx"), None),
    )
    dp_size, ctx_size = mesh.shape["dp"], mesh.shape["ctx"]
    body = local
    if dp_size == 8 and ctx_size == 4:
        body = functools.partial(chip_local, dp_size, ctx_size)
    return jax.shard_map(body, mesh=mesh, in_specs=in_specs, out_specs=out_specs, check_vma=False)
```
